256 devices in a mesh: pool: 4 (over y), ep: 64 (over z, x, core).
Axes of the slice: x: 4, y: 4, z: 8, core: 2. Of those that a mesh axis runs over, the one named last changes fastest.
Arguments:
- residual: bfloat16 [2048, 4096], P(('pool', 'ep')), may hold values from -6 to 6
- queries: bfloat16 [2048, 8192], P(('pool', 'ep')), may hold values from -6 to 6
- token_keys: bfloat16 [2048, 512], P(('pool', 'ep')), may hold values from -6 to 6
- token_values: bfloat16 [2048, 512], P(('pool', 'ep')), may hold values from -6 to 6
- resident_cache: bfloat16 [2048, 2, 64, 512], P(('pool', 'ep')), may hold values from -6 to 6
- pool_block_cache: bfloat16 [64, 128, 2, 16, 512], P('ep', 'pool'), may hold values from -6 to 6
- block_table: int32 [2048, 4], P(('pool', 'ep')), may hold values from 0 to 127, as said below
- resumed: int32 [2048], P(('pool', 'ep')), may hold values from 0 to 1, as said below
- lengths: int32 [2048], P(('pool', 'ep')), may hold values from 2 to 64
- out_proj: bfloat16 [8192, 4096], P('ep'), may hold values from -0.0625 to 0.0625
- norm_gain: bfloat16 [4096], replicated, may hold values from 0.25 to 1.75
- expert_ids: int32 [2048, 8], P(('pool', 'ep')), may hold values from 0 to 63, all different within a row; in each aligned block of 8 rows (0 to 7, 8 to 15, ...) at most 2 rows name the same one
- route_scores: float32 [2048, 8], P(('pool', 'ep')), may hold values from 0.05 to 1
- expert_gate: bfloat16 [64, 4096, 1536], P('ep', None, 'pool'), may hold values from -0.09375 to 0.09375
- expert_up: bfloat16 [64, 4096, 1536], P('ep', None, 'pool'), may hold values from -0.09375 to 0.09375
- expert_down: bfloat16 [64, 1536, 4096], P('ep', 'pool'), may hold values from -0.15625 to 0.15625
Outputs:
- attended: bfloat16 [2048, 4096], P(('pool', 'ep'))
- layer_out: bfloat16 [2048, 4096], P(('pool', 'ep'))
The draws below stay inside these ranges and needn't reach their ends.
Inputs may be any that keep to these rules, and one draw needn't show every extreme that they name: `block_table`: entry // 32 is the pool index that holds the block, within the pool of the row's ep index; every row has 1 of its blocks on each pool index. At most 4 rows of one device are resumed; the first device has exactly 4. `expert_ids`: among the rows of one device no expert is named more than 2 times, a bound that some block reaches.
All inputs are finite; a program needn't handle non-finite values.
Results may differ from the reference program's by a relative error of at most 0.012.
Values may be sent and summed in bfloat16 or wider, within the bound.
No kernel may reach another device: no remote copies, remote signals or barrier semaphores. Data moves between devices by JAX's collectives and lax.ppermute only.
A program may use at most 128 MiB of HBM per device.

```python
import math
import jax
import jax.numpy as jnp
import numpy as np
from jax import lax

D = 4096
QUERY_HEADS = 64
KEY_VALUE_HEADS = 4
HEAD_SIZE = 128
FF = 1536
TOPK = 8
ROWS_DEV = 8
CONTEXT_LIMIT = 64
BLOCK_POSITIONS = 16
SLOTS = 32
RES_MOST = 4
NB = 4
DECODE_ROWS = 2048
EXPERTS = 64
POOL_BLOCK_TOTAL = 128
CAP = 2
N_POOL = 4
N_EP = 64


def draw_queries(key, part):
    key = jax.random.fold_in(key, 11)
    value_rows = jnp.clip(jax.random.normal(key, (DECODE_ROWS, QUERY_HEADS * HEAD_SIZE), jnp.float32), -6.0, 6.0)
    return value_rows.astype(jnp.bfloat16)


def draw_resident_cache(key, part):
    key = jax.random.fold_in(key, 12)
    value_rows = jnp.clip(jax.random.normal(key, (DECODE_ROWS, 2, CONTEXT_LIMIT, KEY_VALUE_HEADS * HEAD_SIZE), jnp.float32), -6.0, 6.0)
    return value_rows.astype(jnp.bfloat16)


def draw_resumed(key, part):
    key = jax.random.fold_in(key, 21)
    leading_key, second_key = jax.random.split(key)
    device_count = DECODE_ROWS // ROWS_DEV
    counts = jax.random.randint(leading_key, (device_count,), 0, RES_MOST + 1)
    counts = counts.at[0].set(RES_MOST)
    offsets = jax.random.randint(second_key, (device_count,), 0, ROWS_DEV)
    placed = (jnp.arange(ROWS_DEV)[None, :] + offsets[:, None]) % ROWS_DEV
    return (placed < counts[:, None]).astype(jnp.int32).reshape(DECODE_ROWS)


def draw_block_table(key, part):
    key = jax.random.fold_in(key, 22)
    leading_key, second_key = jax.random.split(key)
    turns = jax.random.randint(leading_key, (DECODE_ROWS, 1), 0, N_POOL)
    holder = (jnp.arange(NB)[None, :] + turns) % N_POOL
    within = jax.random.randint(second_key, (DECODE_ROWS, NB), 0, SLOTS)
    return (holder * SLOTS + within).astype(jnp.int32)


def place_ends(array, own_key, least, high):
    extent = array.shape
    index_at = [jax.random.randint(jax.random.fold_in(own_key, axis), (), 0, extent[axis]) for axis in range(len(extent))]
    array = array.at[tuple(index_at)].set(least)
    longest = extent.index(max(extent))
    index_at[longest] = (index_at[longest] + 1) % extent[longest]
    return array.at[tuple(index_at)].set(high)


def steps_of(own_key, extent, cuts, least, high):
    def one(dim, parts):
        heights = jax.random.uniform(jax.random.fold_in(jax.random.fold_in(own_key, 6), dim), (parts,), jnp.float32, least / len(cuts), high / len(cuts))
        return jnp.repeat(jnp.exp(heights), extent[dim] // parts).reshape((-1,) + (1,) * (len(extent) - dim - 1))

    level = one(*cuts[0])
    for cut in cuts[1:]:
        level = level * one(*cut)
    return level


def deal_out(stream_key, own, number, rows, count, top, bound, skew):
    order = jax.random.permutation(stream_key, count)
    packed, usual = load_shares(count, rows * top, bound, skew, True), load_shares(count, rows * top, bound, skew, False)
    places = jnp.arange(count)

    def named(sizes, offset_by):
        used = int((sizes > 0).sum())
        fixed = max(1, used // 4)
        passed = fixed + (places - fixed + offset_by * (used - fixed)) % max(1, count - fixed)
        return jnp.zeros((count,), jnp.int32).at[order[jnp.where(places < fixed, places, passed)]].set(jnp.asarray(sizes, jnp.int32))

    sizes = jnp.where(number % 4 == 0, named(packed, number // 4), named(usual, number - number // 4 - 1))
    mixed = jax.random.permutation(jax.random.fold_in(own, 3), count)
    giver, taker = mixed[0:count // 2 * 2:2], mixed[1:count // 2 * 2:2]
    slack = jnp.minimum(sizes[giver] - 1, bound - sizes[taker]) // 2
    slack = jnp.where((giver == order[0]) | (taker == order[0]) | (sizes[taker] == 0), 0, jnp.maximum(slack, 0))
    passed = jax.random.randint(jax.random.fold_in(own, 4), (count // 2,), 0, 1 << 20) % (slack + 1)
    sizes = sizes.at[giver].add(-passed).at[taker].add(passed)
    labels = jnp.searchsorted(jnp.cumsum(sizes), jnp.arange(rows * top), side="right").astype(jnp.int32)
    grid = labels.reshape(top, rows).T
    grid = grid[jax.random.permutation(jax.random.fold_in(own, 1), rows)]
    offset_by = jax.random.randint(jax.random.fold_in(own, 2), (rows, 1), 0, top)
    return jnp.take_along_axis(grid, (jnp.arange(top)[None, :] + offset_by) % top, axis=1)


def load_shares(count, total, bound, slope, full):
    portions = [(1 << 20) // math.isqrt(rank ** slope) + 1 for rank in range(1, count + 1)]
    largest = bound if full else min(bound, max(-(-total // count), total * portions[0] // sum(portions)))
    least = 1 if total - largest >= count - 1 else 0
    given, surplus = [largest] + [least] * (count - 1), total - largest - least * (count - 1)
    while surplus > 0:
        free = [i for i in range(1, count) if given[i] < largest] or [i for i in range(1, count) if given[i] < bound]
        pool, remaining = sum([portions[i] for i in free]), surplus
        for i in free:
            more = min(bound - given[i], max(1, remaining * portions[i] // pool), surplus)
            given[i] = given[i] + more
            surplus = surplus - more
    return np.array(given)


def noise(rng, shape, deviation, limit, cuts=(), held_as=jnp.bfloat16):
    gain = steps_of(rng, shape, cuts, -0.22, 0.18) if cuts else 1.0
    values = jax.random.normal(rng, shape, jnp.float32) * deviation * gain
    return jnp.minimum(jnp.maximum(values, -limit), limit).astype(held_as)


def setup_inputs(seed: int = 0) -> dict:
    key_list = jax.random.split(jax.random.key(seed), 17)
    residual = noise(key_list[0], (DECODE_ROWS, D), 1.0, 6.0, ((0, 256),))
    queries = draw_queries(jax.random.fold_in(key_list[16], 71), 0)
    token_keys = noise(key_list[2], (DECODE_ROWS, KEY_VALUE_HEADS * HEAD_SIZE), 1.0, 6.0, ((0, 256),))
    token_values = noise(key_list[3], (DECODE_ROWS, KEY_VALUE_HEADS * HEAD_SIZE), 1.0, 6.0, ((0, 256),))
    resident_cache = draw_resident_cache(jax.random.fold_in(key_list[16], 71), 0)
    pool_block_cache = noise(key_list[5], (N_EP, POOL_BLOCK_TOTAL, 2, BLOCK_POSITIONS, KEY_VALUE_HEADS * HEAD_SIZE), 1.0, 6.0, ((0, 64), (1, 4)))
    block_table = draw_block_table(jax.random.fold_in(key_list[16], 71), 0)
    resumed = draw_resumed(jax.random.fold_in(key_list[16], 71), 0)
    lengths = place_ends(jax.random.randint(key_list[8], (DECODE_ROWS,), 2, CONTEXT_LIMIT + 1), jax.random.fold_in(key_list[8], 1), 2, CONTEXT_LIMIT).astype(jnp.int32)
    out_proj = noise(key_list[9], (QUERY_HEADS * HEAD_SIZE, D), (QUERY_HEADS * HEAD_SIZE) ** -0.5, 0.0625, ((0, 64),))
    norm_gain = jnp.clip(1.0 + 0.15 * jax.random.normal(key_list[10], (D,), jnp.float32), 0.25, 1.75).astype(jnp.bfloat16)
    expert_ids_keys = jax.random.split(jax.random.fold_in(key_list[11], 1), DECODE_ROWS // ROWS_DEV)
    expert_ids_turns = jax.random.permutation(jax.random.fold_in(key_list[11], 3), DECODE_ROWS // ROWS_DEV)
    expert_ids = jax.vmap(lambda own, number: deal_out(jax.random.fold_in(key_list[11], 2), own, number, ROWS_DEV, EXPERTS, TOPK, CAP, 2))(expert_ids_keys, expert_ids_turns).reshape((DECODE_ROWS, TOPK))
    route_scores = jnp.clip(jnp.exp(math.log(1.0) - 2.9957323 * jax.random.uniform(key_list[12], (DECODE_ROWS, TOPK), jnp.float32) ** steps_of(key_list[12], (DECODE_ROWS, TOPK), ((0, 256),), -0.2, 0.2)), 0.05, 1.0)
    expert_gate = noise(key_list[13], (EXPERTS, D, FF), D ** -0.5, 0.09375, ((0, 64), (2, 4)))
    expert_up = noise(key_list[14], (EXPERTS, D, FF), D ** -0.5, 0.09375, ((0, 64), (2, 4)))
    expert_down = noise(key_list[15], (EXPERTS, FF, D), FF ** -0.5, 0.15625, ((0, 64), (1, 4)))
    return dict(residual=residual, queries=queries, token_keys=token_keys, token_values=token_values, resident_cache=resident_cache, pool_block_cache=pool_block_cache, block_table=block_table, resumed=resumed, lengths=lengths, out_proj=out_proj, norm_gain=norm_gain, expert_ids=expert_ids, route_scores=route_scores, expert_gate=expert_gate, expert_up=expert_up, expert_down=expert_down)


NEG_FILL = -1e+30
NORM_EPSILON = 1e-06

def attend_rows(queries, active_cache, token_keys, token_values, lengths):
    total_rows = queries.shape[0]
    group_query_heads = QUERY_HEADS // KEY_VALUE_HEADS
    query_matrix = queries.reshape(total_rows, KEY_VALUE_HEADS, group_query_heads, HEAD_SIZE).astype(jnp.float32)
    key_portion = active_cache[:, 0].reshape(total_rows, CONTEXT_LIMIT, KEY_VALUE_HEADS, HEAD_SIZE).astype(jnp.float32)
    value_portion = active_cache[:, 1].reshape(total_rows, CONTEXT_LIMIT, KEY_VALUE_HEADS, HEAD_SIZE).astype(jnp.float32)
    self_key = token_keys.reshape(total_rows, KEY_VALUE_HEADS, HEAD_SIZE).astype(jnp.float32)
    self_value = token_values.reshape(total_rows, KEY_VALUE_HEADS, HEAD_SIZE).astype(jnp.float32)
    factor = 1.0 / math.sqrt(HEAD_SIZE)
    scores = jnp.einsum('rkgd,rtkd->rkgt', query_matrix, key_portion) * factor
    own_score = jnp.einsum('rkgd,rkd->rkg', query_matrix, self_key) * factor
    live_mask = (jnp.arange(CONTEXT_LIMIT)[None, :] < lengths[:, None])[:, None, None, :]
    scores = jnp.where(live_mask, scores, NEG_FILL)
    highest = jnp.maximum(lax.optimization_barrier(jnp.max(scores, axis=-1)), own_score)
    raised = jnp.where(live_mask, jnp.exp(scores - highest[..., None]), 0.0)
    own_raised = jnp.exp(own_score - highest)
    denominator = lax.optimization_barrier(jnp.sum(raised, axis=-1)) + own_raised
    weights = (raised / denominator[..., None]).astype(jnp.bfloat16)
    own_weight = (own_raised / denominator).astype(jnp.bfloat16)
    context = jnp.einsum('rkgt,rtkd->rkgd', weights.astype(jnp.float32), value_portion)
    context = context + own_weight.astype(jnp.float32)[..., None] * self_value[:, :, None, :]
    return context.reshape(total_rows, QUERY_HEADS * HEAD_SIZE).astype(jnp.bfloat16)

def reference(residual, queries, token_keys, token_values, resident_cache, pool_block_cache, block_table, resumed, lengths, out_proj, norm_gain, expert_ids, route_scores, expert_gate, expert_up, expert_down):
    total_rows = residual.shape[0]
    column = (jnp.arange(total_rows) // ROWS_DEV % N_EP).astype(jnp.int32)
    loaded_blocks = pool_block_cache[column[:, None], block_table]
    ordered_blocks = jnp.transpose(loaded_blocks, (0, 2, 1, 3, 4)).reshape(total_rows, 2, CONTEXT_LIMIT, KEY_VALUE_HEADS * HEAD_SIZE)
    active_cache = jnp.where(resumed[:, None, None, None] > 0, ordered_blocks, resident_cache)
    context = attend_rows(queries, active_cache, token_keys, token_values, lengths)
    projected = jnp.dot(context, out_proj, preferred_element_type=jnp.float32)
    attended = (residual.astype(jnp.float32) + projected).astype(jnp.bfloat16)
    widened = attended.astype(jnp.float32)
    normed = (widened * lax.rsqrt(lax.optimization_barrier(jnp.mean(widened * widened, axis=-1, keepdims=True)) + NORM_EPSILON) * norm_gain.astype(jnp.float32)).astype(jnp.bfloat16)
    shares = route_scores / lax.optimization_barrier(jnp.sum(route_scores, axis=-1, keepdims=True))
    flat_ids = expert_ids.reshape(-1)
    flat_shares = shares.reshape(-1)
    slot_limit = CAP * N_POOL * N_EP
    quarter = FF // N_POOL

    def one_expert(expert, mixture):
        pair_order = jnp.argsort((flat_ids != expert).astype(jnp.int32), stable=True)[:slot_limit].astype(jnp.int32)
        chosen = flat_ids[pair_order] == expert
        source = pair_order // TOPK
        inputs = normed[source]
        gate_part = jnp.dot(inputs, expert_gate[expert], preferred_element_type=jnp.float32)
        up_part = jnp.dot(inputs, expert_up[expert], preferred_element_type=jnp.float32)
        hidden = (jax.nn.silu(gate_part) * up_part).astype(jnp.bfloat16)
        down_weights = expert_down[expert]
        summed = jnp.zeros((slot_limit, D), jnp.float32)
        for piece_index in range(N_POOL):
            partial_value = jnp.dot(hidden[:, piece_index * quarter:(piece_index + 1) * quarter], down_weights[piece_index * quarter:(piece_index + 1) * quarter], preferred_element_type=jnp.float32)
            summed = summed + lax.optimization_barrier(partial_value.astype(jnp.bfloat16)).astype(jnp.float32)
        output = lax.optimization_barrier(summed.astype(jnp.bfloat16)).astype(jnp.float32)
        weight = jnp.where(chosen, flat_shares[pair_order], 0.0)
        return mixture.at[source].add(weight[:, None] * output)
    mixture = lax.fori_loop(0, EXPERTS, one_expert, jnp.zeros((total_rows, D), jnp.float32))
    layer_out = (attended.astype(jnp.float32) + mixture).astype(jnp.bfloat16)
    return (attended, layer_out)
```

```python
import functools
import math

import jax
import jax.numpy as jnp
import numpy as np
from jax import lax
from jax.experimental import pallas as pl
from jax.experimental.pallas import tpu as pltpu
from jax.sharding import PartitionSpec as P

D = 4096
QUERY_HEADS = 64
KEY_VALUE_HEADS = 4
GROUP = QUERY_HEADS // KEY_VALUE_HEADS
HEAD_SIZE = 128
WIDE = KEY_VALUE_HEADS * HEAD_SIZE
CONTEXT_LIMIT = 64
BLOCK_POSITIONS = 16
RES_MOST = 4
CAP = 2
ROWS = 8
FACTS = 7
N_POOL = 4
N_Z, N_X, N_CORE = 8, 4, 2
N_PLANE = N_X * N_CORE
N_EP = N_Z * N_PLANE
DEEP = N_PLANE * HEAD_SIZE
CHUNK = D // N_PLANE
PARTS = 4
PART = D // PARTS
FF_PART = 384
STEPS = 2
PER_STEP = PARTS // STEPS
HALF = N_EP // 2 * PARTS * CAP
NORM_EPSILON = 1e-06
NEG_FILL = -1e30
BIG = 48 * 1024 * 1024
MOST = 60 * 1024 * 1024


def shift_pool(value, step):
    return lax.ppermute(value, "pool", [(i, (i + step) % N_POOL) for i in range(N_POOL)])


def shift_ep(value, x=0, core=0):
    pairs = []
    for i in range(N_EP):
        a, b, c = i // N_PLANE, i // N_CORE % N_X, i % N_CORE
        pairs.append((i, a * N_PLANE + (b + x) % N_X * N_CORE + (c + core) % N_CORE))
    return lax.ppermute(value, "ep", pairs)


def whole(shape):
    return pl.BlockSpec(shape, lambda *_: (0,) * len(shape))


def gather_kernel(asked_ref, cache_ref, *refs):
    outs, sems = refs[:N_POOL], refs[N_POOL]
    copies = []
    for d in range(N_POOL):
        for j in range(RES_MOST):
            copy = pltpu.make_async_copy(
                cache_ref.at[asked_ref[d * RES_MOST + j]], outs[d].at[j], sems.at[d * RES_MOST + j]
            )
            copy.start()
            copies.append(copy)
    for copy in copies:
        copy.wait()


def fetch_blocks(cache, block_table, resumed, lengths, pool):
    slots = cache.shape[0]
    live = resumed > 0
    row = jnp.arange(ROWS)
    rank = jnp.sum(jnp.where(row[None, :] < row[:, None], resumed[None, :], 0), axis=1)
    rank = jnp.clip(rank, 0, RES_MOST - 1)
    holder = block_table // slots
    within = block_table % slots
    from_me = (pool + jnp.arange(N_POOL)) % N_POOL
    at_holder = holder[None] == from_me[:, None, None]
    at_rank = live[None, :] & (rank[None, :] == jnp.arange(RES_MOST)[:, None])
    chosen = at_holder[:, None] & at_rank[None, :, :, None]
    wanted = jnp.sum(jnp.where(chosen, within[None, None], 0), axis=(2, 3))
    start = jnp.arange(N_POOL) * BLOCK_POSITIONS
    place = jnp.sum(jnp.where(at_holder, start[None, None, :], 0), axis=2).T
    place = jnp.where(live[:, None], place, start[None, :])
    asked = jnp.concatenate([wanted[0]] + [shift_pool(wanted[d], d) for d in range(1, N_POOL)])
    asked = jnp.clip(asked, 0, slots - 1)
    shape = jax.ShapeDtypeStruct((RES_MOST,) + cache.shape[1:], jnp.bfloat16)
    gathered = pl.pallas_call(
        gather_kernel,
        grid_spec=pltpu.PrefetchScalarGridSpec(
            num_scalar_prefetch=1,
            grid=(1,),
            in_specs=[pl.BlockSpec(memory_space=pl.ANY)],
            out_specs=[whole((RES_MOST,) + cache.shape[1:])] * N_POOL,
            scratch_shapes=[pltpu.SemaphoreType.DMA((N_POOL * RES_MOST,))],
        ),
        out_shape=[shape] * N_POOL,
        cost_estimate=pl.CostEstimate(flops=0, bytes_accessed=1 << 20, transcendentals=0),
    )(asked, cache)
    blocks = [gathered[0]] + [shift_pool(gathered[d], -d) for d in range(1, N_POOL)]
    facts = jnp.concatenate([rank[:, None], resumed[:, None], lengths[:, None], place], axis=1)
    return blocks, facts.reshape(-1)


def attention_kernel(facts_ref, query_ref, key_ref, value_ref, resident_ref, b0, b1, b2, b3, out_ref):
    wider = CONTEXT_LIMIT + 16
    lane = lax.broadcasted_iota(jnp.int32, (1, wider), 1)
    head_of = lax.broadcasted_iota(jnp.int32, (QUERY_HEADS, WIDE), 0) // GROUP
    block_of = lax.broadcasted_iota(jnp.int32, (QUERY_HEADS, WIDE), 1) // HEAD_SIZE
    diagonal = head_of == block_of
    first = lax.broadcasted_iota(jnp.int32, (16, WIDE), 0) == 0
    factor = 1.0 / math.sqrt(HEAD_SIZE)
    results = []
    for row in range(ROWS):
        rank, resumed, length, *place = [facts_ref[row * FACTS + i] for i in range(FACTS)]
        is_resumed = resumed > 0

        def of_kind(kind, own_ref):
            loaded = jnp.concatenate([b[rank, kind] for b in (b0, b1, b2, b3)], axis=0)
            cached = jnp.where(is_resumed, loaded, resident_ref[row, kind])
            own = jnp.where(first, own_ref[row : row + 1, :].astype(jnp.float32), 0.0)
            return jnp.concatenate([cached, own.astype(jnp.bfloat16)], axis=0)

        keys, values = of_kind(0, key_ref), of_kind(1, value_ref)
        position = lane % BLOCK_POSITIONS
        for i in range(N_POOL):
            position = position + jnp.where(lane // BLOCK_POSITIONS == i, place[i], 0)
        live = ((lane < CONTEXT_LIMIT) & (position < length)) | (lane == CONTEXT_LIMIT)
        query = query_ref[row]
        query = jnp.where(diagonal, jnp.concatenate([query] * KEY_VALUE_HEADS, axis=1), 0)
        scores = lax.dot_general(
            query.astype(jnp.bfloat16), keys, (((1,), (1,)), ((), ())), preferred_element_type=jnp.float32
        )
        scores = jnp.where(live, scores * factor, NEG_FILL)
        highest = jnp.max(scores, axis=1, keepdims=True)
        raised = jnp.where(live, jnp.exp(scores - highest), 0.0)
        weights = (raised / jnp.sum(raised, axis=1, keepdims=True)).astype(jnp.bfloat16)
        spread = jnp.dot(weights, values, preferred_element_type=jnp.float32)
        results.append(
            jnp.concatenate(
                [
                    spread[k * GROUP : (k + 1) * GROUP, k * HEAD_SIZE : (k + 1) * HEAD_SIZE]
                    for k in range(KEY_VALUE_HEADS)
                ],
                axis=0,
            )
        )
    by_head = jnp.swapaxes(jnp.stack(results), 0, 1)
    for z in range(N_Z):
        plane = jnp.concatenate([by_head[z * N_PLANE + h] for h in range(N_PLANE)], axis=1)
        copies = jnp.concatenate([plane] * N_X, axis=0).astype(jnp.bfloat16)
        out_ref[z * N_X * ROWS : (z + 1) * N_X * ROWS, :] = copies


def attend(queries, token_keys, token_values, resident, blocks, facts):
    block = whole(blocks[0].shape)
    sent = N_Z * N_X * ROWS
    return pl.pallas_call(
        attention_kernel,
        grid_spec=pltpu.PrefetchScalarGridSpec(
            num_scalar_prefetch=1,
            grid=(1,),
            in_specs=[
                whole((ROWS, QUERY_HEADS, HEAD_SIZE)),
                whole((ROWS, WIDE)),
                whole((ROWS, WIDE)),
                whole(resident.shape),
                block,
                block,
                block,
                block,
            ],
            out_specs=whole((sent, DEEP)),
        ),
        out_shape=jax.ShapeDtypeStruct((sent, DEEP), jnp.bfloat16),
        compiler_params=pltpu.CompilerParams(vmem_limit_bytes=MOST),
        cost_estimate=pl.CostEstimate(flops=1 << 28, bytes_accessed=3 << 20, transcendentals=1 << 16),
    )(
        facts, queries.reshape(ROWS, QUERY_HEADS, HEAD_SIZE), token_keys, token_values, resident, *blocks
    )


def pair_projection(out_proj, core):
    columns = N_X * CHUNK
    mine = lax.dynamic_slice_in_dim(out_proj, core * columns, columns, 1)
    other = lax.dynamic_slice_in_dim(out_proj, (1 - core) * columns, columns, 1)
    came = shift_ep(other, core=1)
    both = jnp.where(core == 0, jnp.stack([mine, came]), jnp.stack([came, mine]))
    return both.reshape(N_CORE * HEAD_SIZE, columns)


def spread_projection(pair, x):
    pieces = []
    for d in range(N_X):
        piece = lax.dynamic_slice_in_dim(pair, (x + d) % N_X * CHUNK, CHUNK, 1)
        pieces.append(piece if d == 0 else shift_ep(piece, x=d))
    return pieces


def project_kernel(at_ref, mine_ref, other_ref, w0, w1, w2, w3, out_ref):
    x, core = at_ref[0], at_ref[1]
    width = N_CORE * HEAD_SIZE
    products = []
    for rows_ref in (mine_ref, other_ref):
        total = jnp.zeros((rows_ref.shape[0], CHUNK), jnp.float32)
        for d, w_ref in enumerate((w0, w1, w2, w3)):
            source = (x + N_X - d) % N_X
            columns = pl.ds(pl.multiple_of(source * width, width), width)
            total = total + jnp.dot(rows_ref[:, columns], w_ref[...], preferred_element_type=jnp.float32)
        products.append(total.reshape(N_Z * N_X, ROWS, CHUNK))
    mine, other = products
    first = jnp.where(core == 0, mine, other)
    second = jnp.where(core == 0, other, mine)
    both = jnp.concatenate([first, second], axis=1)
    out_ref[...] = both.reshape(N_EP * ROWS, CHUNK).astype(jnp.bfloat16)


def project(context, pieces, x, core):
    same_core = [[i * N_CORE + c for i in range(N_Z * N_X)] for c in range(N_CORE)]
    mine = lax.all_to_all(
        context.reshape(N_Z * N_X, ROWS, DEEP),
        "ep", split_axis=0, concat_axis=0, axis_index_groups=same_core, tiled=True,
    ).reshape(N_Z * N_X * ROWS, DEEP)
    other = shift_ep(mine, core=1)
    product = pl.pallas_call(
        project_kernel,
        grid_spec=pltpu.PrefetchScalarGridSpec(
            num_scalar_prefetch=1,
            grid=(1,),
            in_specs=[whole(mine.shape)] * 2 + [whole(pieces[0].shape)] * N_X,
            out_specs=whole((N_EP * ROWS, CHUNK)),
        ),
        out_shape=jax.ShapeDtypeStruct((N_EP * ROWS, CHUNK), jnp.bfloat16),
        compiler_params=pltpu.CompilerParams(vmem_limit_bytes=BIG),
    )(jnp.stack([x, core]).astype(jnp.int32), mine, other, *pieces)
    summands = lax.all_to_all(
        product.reshape(N_EP, ROWS, CHUNK), "ep", split_axis=0, concat_axis=0, tiled=True
    )
    return summands.reshape(N_EP * ROWS, CHUNK)


def dispatch_kernel(summand_ref, residual_ref, gain_ref, pick_ref, attended_ref, out_ref):
    total = summand_ref[...].astype(jnp.float32).reshape(N_Z, N_PLANE * ROWS, CHUNK).sum(axis=0)
    columns = []
    for chunk in range(N_PLANE):
        source = chunk % N_X * N_CORE + chunk // N_X
        columns.append(total[source * ROWS : (source + 1) * ROWS])
    projected = jnp.concatenate(columns, axis=1)
    attended = (residual_ref[...].astype(jnp.float32) + projected).astype(jnp.bfloat16)
    attended_ref[...] = attended
    widened = attended.astype(jnp.float32)
    mean = jnp.sum(widened * widened, axis=1, keepdims=True) * (1.0 / D)
    normed = widened * lax.rsqrt(mean + NORM_EPSILON) * gain_ref[...].astype(jnp.float32)
    stacked = jnp.concatenate([normed[:, j * PART : (j + 1) * PART] for j in range(PARTS)], axis=0)
    out_ref[...] = jnp.dot(
        pick_ref[...], stacked.astype(jnp.bfloat16), preferred_element_type=jnp.float32
    ).astype(jnp.bfloat16)


def expert_kernel(layout, order_ref, *refs):
    count = len(layout)
    ins, (gate_ref, up_ref, down_ref) = refs[:count], refs[count : count + 3]
    outs = refs[count + 3 : 2 * count + 3]
    tokens, gate_sum, up_sum, hidden, results = refs[2 * count + 3 :]
    halves = [(i, h) for i, n in enumerate(layout) for h in range(n)]
    per_half = HALF // PARTS
    step = pl.program_id(0)

    @pl.when(step == 0)
    def _():
        for at, (i, h) in enumerate(halves):
            block = jnp.dot(
                order_ref[...], ins[i][h * HALF : (h + 1) * HALF, :], preferred_element_type=jnp.float32
            ).astype(jnp.bfloat16)
            for j in range(PARTS):
                tokens[j, at * per_half : (at + 1) * per_half, :] = block[j * per_half : (j + 1) * per_half]

    for i in range(STEPS):

        @pl.when(step == i)
        def _():
            gate = up = None
            for at in range(PER_STEP):
                part = tokens[i * PER_STEP + at]
                depth = slice(at * PART, (at + 1) * PART)
                more = jnp.dot(part, gate_ref[depth, :], preferred_element_type=jnp.float32)
                gate = more if gate is None else gate + more
                more = jnp.dot(part, up_ref[depth, :], preferred_element_type=jnp.float32)
                up = more if up is None else up + more
            if i > 0:
                gate, up = gate + gate_sum[...], up + up_sum[...]
            if i < STEPS - 1:
                gate_sum[...], up_sum[...] = gate, up
            else:
                hidden[...] = (gate * (1.0 / (1.0 + jnp.exp(-gate))) * up).astype(jnp.bfloat16)

        @pl.when(step == STEPS + i)
        def _():
            for at in range(PER_STEP):
                results[i * PER_STEP + at] = jnp.dot(
                    hidden[...], down_ref[:, at * PART : (at + 1) * PART], preferred_element_type=jnp.float32
                ).astype(jnp.bfloat16)

    @pl.when(step == 2 * STEPS - 1)
    def _():
        for at, (i, h) in enumerate(halves):
            block = jnp.concatenate(
                [results[j, at * per_half : (at + 1) * per_half, :] for j in range(PARTS)], axis=0
            )
            outs[i][h * HALF : (h + 1) * HALF, :] = lax.dot_general(
                order_ref[...], block, (((0,), (0,)), ((), ())), preferred_element_type=jnp.float32
            ).astype(jnp.bfloat16)


def expert(arrays, w_gate, w_up, w_down, order):
    layout = [a.shape[0] // HALF for a in arrays]
    rows = sum(layout) * HALF // PARTS
    span = PER_STEP * PART
    gate_spec = pl.BlockSpec((span, FF_PART), lambda i: (jnp.minimum(i, STEPS - 1), 0))
    down_spec = pl.BlockSpec((FF_PART, span), lambda i: (0, jnp.maximum(i - STEPS, 0)))
    return pl.pallas_call(
        functools.partial(expert_kernel, layout),
        grid=(2 * STEPS,),
        in_specs=[whole(order.shape)] + [whole(a.shape) for a in arrays] + [gate_spec, gate_spec, down_spec],
        out_specs=[whole(a.shape) for a in arrays],
        out_shape=[jax.ShapeDtypeStruct(a.shape, jnp.bfloat16) for a in arrays],
        scratch_shapes=[
            pltpu.VMEM((PARTS, rows, PART), jnp.bfloat16),
            pltpu.VMEM((rows, FF_PART), jnp.float32),
            pltpu.VMEM((rows, FF_PART), jnp.float32),
            pltpu.VMEM((rows, FF_PART), jnp.bfloat16),
            pltpu.VMEM((PARTS, rows, PART), jnp.bfloat16),
        ],
        compiler_params=pltpu.CompilerParams(vmem_limit_bytes=BIG),
        cost_estimate=pl.CostEstimate(
            flops=6 * rows * D * FF_PART, bytes_accessed=6 * D * FF_PART + 4 * rows * D, transcendentals=0
        ),
    )(order, *arrays, w_gate, w_up, w_down)


def finish_kernel(mix_ref, returned_ref, attended_ref, out_ref):
    summed = jnp.dot(mix_ref[...], returned_ref[...], preferred_element_type=jnp.float32)
    wide = PARTS * ROWS
    summed = summed[:wide] + summed[wide : 2 * wide] + summed[2 * wide :]
    mixture = jnp.concatenate([summed[j * ROWS : (j + 1) * ROWS] for j in range(PARTS)], axis=1)
    out_ref[...] = (attended_ref[...].astype(jnp.float32) + mixture).astype(jnp.bfloat16)


def routes(expert_ids, route_scores):
    shares = route_scores / jnp.sum(route_scores, axis=1, keepdims=True)
    named = expert_ids[:, :, None] == jnp.arange(N_EP)[None, None, :]
    hit = jnp.any(named, axis=1)
    share = jnp.sum(jnp.where(named, shares[:, :, None], 0.0), axis=1)
    row = jnp.arange(ROWS)
    earlier = row[None, :, None] < row[:, None, None]
    before = jnp.sum(jnp.where(earlier & hit[None], 1, 0), axis=1)
    slot = hit[:, :, None] & (before[:, :, None] == jnp.arange(CAP))
    same = jnp.arange(PARTS)[:, None] == jnp.arange(PARTS)[None, :]
    pick = jnp.where(
        slot.transpose(1, 2, 0)[:, None, :, None, :] & same[None, :, None, :, None], 1.0, 0.0
    ).reshape(N_EP * PARTS * CAP, PARTS * ROWS)
    mix = jnp.where(
        slot[None, :, :, None, :] & same[:, None, None, :, None], share[None, :, :, None, None], 0.0
    ).reshape(PARTS * ROWS, N_EP * PARTS * CAP)
    high = lax.reduce_precision(mix, 8, 7)
    middle = lax.reduce_precision(mix - high, 8, 7)
    low = mix - high - middle
    return pick.astype(jnp.bfloat16), jnp.concatenate([high, middle, low]).astype(jnp.bfloat16)


def order_matrix():
    half = N_EP // 2
    message = np.arange(HALF).reshape(half, PARTS, CAP)
    token = message.transpose(1, 0, 2).reshape(-1)
    return (token[:, None] == np.arange(HALF)[None, :]).astype(jnp.bfloat16)


def shards(
    residual,
    queries,
    token_keys,
    token_values,
    resident_cache,
    pool_block_cache,
    block_table,
    resumed,
    lengths,
    out_proj,
    norm_gain,
    expert_ids,
    route_scores,
    expert_gate,
    expert_up,
    expert_down,
):
    pool = lax.axis_index("pool")
    ep = lax.axis_index("ep")
    x, core = ep // N_CORE % N_X, ep % N_CORE

    blocks, facts = fetch_blocks(pool_block_cache[0], block_table, resumed, lengths, pool)
    pair = pair_projection(out_proj, core)
    blocks[1], pair = lax.optimization_barrier((blocks[1], pair))
    pieces = spread_projection(pair, x)
    pick, mix = routes(expert_ids, route_scores)
    context = attend(queries, token_keys, token_values, resident_cache, blocks, facts)
    context, *pieces = lax.optimization_barrier((context, *pieces))
    summands = project(context, pieces, x, core)
    message = (N_EP * PARTS * CAP, PART)
    attended, outgoing = pl.pallas_call(
        dispatch_kernel,
        out_shape=[
            jax.ShapeDtypeStruct((ROWS, D), jnp.bfloat16),
            jax.ShapeDtypeStruct(message, jnp.bfloat16),
        ],
        compiler_params=pltpu.CompilerParams(vmem_limit_bytes=BIG),
    )(summands, residual, norm_gain.reshape(1, D), pick)

    def exchange(rows):
        parted = rows.reshape(N_EP, PARTS * CAP, PART)
        return lax.all_to_all(parted, "ep", split_axis=0, concat_axis=0, tiled=True).reshape(message)

    weights = (expert_gate[0], expert_up[0], expert_down[0], jnp.asarray(order_matrix()))
    mine = exchange(outgoing)
    left, right = shift_pool(mine, 1), shift_pool(mine, -1)
    (own,) = expert([mine], *weights)
    left, right, own = lax.optimization_barrier((left, right, own))
    far_a, far_b = shift_pool(right[:HALF], -1), shift_pool(left[HALF:], 1)
    to_left, to_right = expert([left, right], *weights)
    right_b, left_a = shift_pool(to_right[HALF:], 1), shift_pool(to_left[:HALF], -1)
    far_a, far_b, to_left, to_right = lax.optimization_barrier((far_a, far_b, to_left, to_right))
    to_far_a, to_far_b = expert([far_a, far_b], *weights)
    over_a, over_b = shift_pool(to_far_a, 1), shift_pool(to_far_b, -1)

    def wide(value):
        return value.astype(jnp.float32)

    base_a, base_b = wide(own[:HALF]) + wide(left_a), wide(own[HALF:]) + wide(right_b)
    over_a, over_b, base_a, base_b = lax.optimization_barrier((over_a, over_b, base_a, base_b))
    right_a = shift_pool((wide(to_right[:HALF]) + wide(over_a)).astype(jnp.bfloat16), 1)
    left_b = shift_pool((wide(to_left[HALF:]) + wide(over_b)).astype(jnp.bfloat16), -1)
    summed = jnp.concatenate([base_a + wide(right_a), base_b + wide(left_b)]).astype(jnp.bfloat16)
    returned = exchange(summed)
    layer_out = pl.pallas_call(
        finish_kernel,
        out_shape=jax.ShapeDtypeStruct((ROWS, D), jnp.bfloat16),
        compiler_params=pltpu.CompilerParams(vmem_limit_bytes=BIG),
    )(mix, returned, attended)
    return (attended, layer_out)


def solution(mesh):
    placed = (
        P(("pool", "ep"), None),
        P(("pool", "ep"), None),
        P(("pool", "ep"), None),
        P(("pool", "ep"), None),
        P(("pool", "ep"), None, None, None),
        P("ep", "pool", None, None, None),
        P(("pool", "ep"), None),
        P(("pool", "ep")),
        P(("pool", "ep")),
        P("ep", None),
        P(),
        P(("pool", "ep"), None),
        P(("pool", "ep"), None),
        P("ep", None, "pool"),
        P("ep", None, "pool"),
        P("ep", "pool", None),
    )
    return jax.shard_map(
        shards,
        mesh=mesh,
        in_specs=placed,
        out_specs=(P(("pool", "ep"), None), P(("pool", "ep"), None)),
        check_vma=False,
    )
```

```python
import functools
import math

import jax
import jax.numpy as jnp
import numpy as np
from jax import lax
from jax.experimental import pallas as pl
from jax.experimental.pallas import tpu as pltpu
from jax.sharding import PartitionSpec as P

D = 4096
QUERY_HEADS = 64
KEY_VALUE_HEADS = 4
GROUP = QUERY_HEADS // KEY_VALUE_HEADS
HEAD_SIZE = 128
WIDE = KEY_VALUE_HEADS * HEAD_SIZE
CONTEXT_LIMIT = 64
BLOCK_POSITIONS = 16
RES_MOST = 4
CAP = 2
ROWS = 8
FACTS = 7
N_POOL = 4
N_Z, N_X, N_CORE = 8, 4, 2
N_PLANE = N_X * N_CORE
N_EP = N_Z * N_PLANE
DEEP = N_PLANE * HEAD_SIZE
CHUNK = D // N_PLANE
PARTS = 4
PART = D // PARTS
FF_PART = 384
STEPS = 2
PER_STEP = PARTS // STEPS
HALF = N_EP // 2 * PARTS * CAP
NORM_EPSILON = 1e-06
NEG_FILL = -1e30
BIG = 48 * 1024 * 1024
MOST = 60 * 1024 * 1024


def shift_pool(value, step):
    return lax.ppermute(value, "pool", [(i, (i + step) % N_POOL) for i in range(N_POOL)])


def shift_ep(value, x=0, core=0):
    pairs = []
    for i in range(N_EP):
        a, b, c = i // N_PLANE, i // N_CORE % N_X, i % N_CORE
        pairs.append((i, a * N_PLANE + (b + x) % N_X * N_CORE + (c + core) % N_CORE))
    return lax.ppermute(value, "ep", pairs)


def whole(shape):
    return pl.BlockSpec(shape, lambda *_: (0,) * len(shape))


def gather_kernel(asked_ref, cache_ref, *refs):
    outs, sems = refs[:N_POOL], refs[N_POOL]
    copies = []
    for d in range(N_POOL):
        for j in range(RES_MOST):
            copy = pltpu.make_async_copy(
                cache_ref.at[asked_ref[d * RES_MOST + j]], outs[d].at[j], sems.at[d * RES_MOST + j]
            )
            copy.start()
            copies.append(copy)
    for copy in copies:
        copy.wait()


def fetch_blocks(cache, block_table, resumed, lengths, queries, pool):
    slots = cache.shape[0]
    live = resumed > 0
    row = jnp.arange(ROWS)
    rank = jnp.sum(jnp.where(row[None, :] < row[:, None], resumed[None, :], 0), axis=1)
    rank = jnp.clip(rank, 0, RES_MOST - 1)
    holder = block_table // slots
    within = block_table % slots
    from_me = (pool + jnp.arange(N_POOL)) % N_POOL
    at_holder = holder[None] == from_me[:, None, None]
    at_rank = live[None, :] & (rank[None, :] == jnp.arange(RES_MOST)[:, None])
    chosen = at_holder[:, None] & at_rank[None, :, :, None]
    wanted = jnp.sum(jnp.where(chosen, within[None, None], 0), axis=(2, 3))
    start = jnp.arange(N_POOL) * BLOCK_POSITIONS
    place = jnp.sum(jnp.where(at_holder, start[None, None, :], 0), axis=2).T
    place = jnp.where(live[:, None], place, start[None, :])
    asked = jnp.concatenate([wanted[0]] + [shift_pool(wanted[d], d) for d in range(1, N_POOL)])
    asked = jnp.clip(asked, 0, slots - 1)
    facts = jnp.concatenate([rank[:, None], resumed[:, None], lengths[:, None], place], axis=1).reshape(-1)
    queries = queries.reshape(ROWS, QUERY_HEADS, HEAD_SIZE)
    asked, facts, queries = lax.optimization_barrier((asked, facts, queries))
    shape = jax.ShapeDtypeStruct((RES_MOST,) + cache.shape[1:], jnp.bfloat16)
    gathered = pl.pallas_call(
        gather_kernel,
        grid_spec=pltpu.PrefetchScalarGridSpec(
            num_scalar_prefetch=1,
            grid=(1,),
            in_specs=[pl.BlockSpec(memory_space=pl.ANY)],
            out_specs=[whole((RES_MOST,) + cache.shape[1:])] * N_POOL,
            scratch_shapes=[pltpu.SemaphoreType.DMA((N_POOL * RES_MOST,))],
        ),
        out_shape=[shape] * N_POOL,
        cost_estimate=pl.CostEstimate(flops=0, bytes_accessed=1 << 20, transcendentals=0),
    )(asked, cache)
    blocks = [gathered[0]] + [shift_pool(gathered[d], -d) for d in range(1, N_POOL)]
    return blocks, facts, queries, asked


def attention_kernel(facts_ref, query_ref, key_ref, value_ref, resident_ref, b0, b1, b2, b3, out_ref):
    wider = CONTEXT_LIMIT + 16
    lane = lax.broadcasted_iota(jnp.int32, (1, wider), 1)
    head_of = lax.broadcasted_iota(jnp.int32, (QUERY_HEADS, WIDE), 0) // GROUP
    block_of = lax.broadcasted_iota(jnp.int32, (QUERY_HEADS, WIDE), 1) // HEAD_SIZE
    diagonal = head_of == block_of
    first = lax.broadcasted_iota(jnp.int32, (16, WIDE), 0) == 0
    factor = 1.0 / math.sqrt(HEAD_SIZE)
    results = []
    for row in range(ROWS):
        rank, resumed, length, *place = [facts_ref[row * FACTS + i] for i in range(FACTS)]
        is_resumed = resumed > 0

        def of_kind(kind, own_ref):
            loaded = jnp.concatenate([b[rank, kind] for b in (b0, b1, b2, b3)], axis=0)
            cached = jnp.where(is_resumed, loaded, resident_ref[row, kind])
            own = jnp.where(first, own_ref[row : row + 1, :].astype(jnp.float32), 0.0)
            return jnp.concatenate([cached, own.astype(jnp.bfloat16)], axis=0)

        keys, values = of_kind(0, key_ref), of_kind(1, value_ref)
        position = lane % BLOCK_POSITIONS
        for i in range(N_POOL):
            position = position + jnp.where(lane // BLOCK_POSITIONS == i, place[i], 0)
        live = ((lane < CONTEXT_LIMIT) & (position < length)) | (lane == CONTEXT_LIMIT)
        query = query_ref[row]
        query = jnp.where(diagonal, jnp.concatenate([query] * KEY_VALUE_HEADS, axis=1), 0)
        scores = lax.dot_general(
            query.astype(jnp.bfloat16), keys, (((1,), (1,)), ((), ())), preferred_element_type=jnp.float32
        )
        scores = jnp.where(live, scores * factor, NEG_FILL)
        highest = jnp.max(scores, axis=1, keepdims=True)
        raised = jnp.where(live, jnp.exp(scores - highest), 0.0)
        weights = (raised / jnp.sum(raised, axis=1, keepdims=True)).astype(jnp.bfloat16)
        spread = jnp.dot(weights, values, preferred_element_type=jnp.float32)
        results.append(
            jnp.concatenate(
                [
                    spread[k * GROUP : (k + 1) * GROUP, k * HEAD_SIZE : (k + 1) * HEAD_SIZE]
                    for k in range(KEY_VALUE_HEADS)
                ],
                axis=0,
            )
        )
    by_head = jnp.swapaxes(jnp.stack(results), 0, 1)
    planes = [
        jnp.concatenate([by_head[z * N_PLANE + h] for h in range(N_PLANE)], axis=1) for z in range(N_Z)
    ]
    out_ref[...] = jnp.concatenate(planes, axis=0).astype(jnp.bfloat16)


def attend(queries, token_keys, token_values, resident, blocks, facts):
    block = whole(blocks[0].shape)
    sent = N_Z * ROWS
    return pl.pallas_call(
        attention_kernel,
        grid_spec=pltpu.PrefetchScalarGridSpec(
            num_scalar_prefetch=1,
            grid=(1,),
            in_specs=[
                whole((ROWS, QUERY_HEADS, HEAD_SIZE)),
                whole((ROWS, WIDE)),
                whole((ROWS, WIDE)),
                whole(resident.shape),
                block,
                block,
                block,
                block,
            ],
            out_specs=whole((sent, DEEP)),
        ),
        out_shape=jax.ShapeDtypeStruct((sent, DEEP), jnp.bfloat16),
        compiler_params=pltpu.CompilerParams(vmem_limit_bytes=MOST),
        cost_estimate=pl.CostEstimate(flops=1 << 28, bytes_accessed=3 << 20, transcendentals=1 << 16),
    )(
        facts, queries, token_keys, token_values, resident, *blocks
    )


def pair_projection(out_proj, core):
    columns = N_X * CHUNK
    mine = lax.dynamic_slice_in_dim(out_proj, core * columns, columns, 1)
    other = lax.dynamic_slice_in_dim(out_proj, (1 - core) * columns, columns, 1)
    came = shift_ep(other, core=1)
    both = jnp.where(core == 0, jnp.stack([mine, came]), jnp.stack([came, mine]))
    return both.reshape(N_CORE * HEAD_SIZE, columns)


def cut_projection(pair, x):
    return [lax.dynamic_slice_in_dim(pair, (x + d) % N_X * CHUNK, CHUNK, 1) for d in range(N_X)]


def join_kernel(*refs):
    refs[-1][...] = jnp.concatenate([r[...] for r in refs[:-1]], axis=0)


def project_kernel(at_ref, mine_ref, other_ref, w0, w1, w2, w3, out_ref):
    x, core = at_ref[0], at_ref[1]
    width = N_CORE * HEAD_SIZE
    rows = N_Z * ROWS
    total = jnp.zeros((2 * N_X * rows, CHUNK), jnp.float32)
    for d, w_ref in enumerate((w0, w1, w2, w3)):
        source = (x + N_X - d) % N_X
        columns = pl.ds(pl.multiple_of(source * width, width), width)
        taken = jnp.concatenate([mine_ref[:, columns], other_ref[:, columns]], axis=0)
        total = total + jnp.dot(taken, w_ref[...], preferred_element_type=jnp.float32)
    for d in range(N_X):
        mine = total[d * rows : (d + 1) * rows].reshape(N_Z, ROWS, CHUNK)
        other = total[(N_X + d) * rows : (N_X + d + 1) * rows].reshape(N_Z, ROWS, CHUNK)
        first = jnp.where(core == 0, mine, other)
        second = jnp.where(core == 0, other, mine)
        both = jnp.concatenate([first, second], axis=1).astype(jnp.bfloat16)
        out_ref[:, pl.ds((x + N_X - d) % N_X, 1)] = both.reshape(N_Z, 1, N_CORE * ROWS, CHUNK)


def project(context, pieces, x, core):
    columns = [[z * N_PLANE + i for z in range(N_Z)] for i in range(N_PLANE)]
    local = lax.all_to_all(
        context.reshape(N_Z, ROWS, DEEP),
        "ep", split_axis=0, concat_axis=0, axis_index_groups=columns, tiled=True,
    ).reshape(N_Z * ROWS, DEEP)
    far = [shift_ep(local, x=d) for d in range(1, N_X)]
    mine = pl.pallas_call(
        join_kernel,
        out_shape=jax.ShapeDtypeStruct((N_X * N_Z * ROWS, DEEP), jnp.bfloat16),
        compiler_params=pltpu.CompilerParams(vmem_limit_bytes=BIG),
    )(local, *far)
    operands = [mine, shift_ep(mine, core=1), *pieces]
    shape = (N_Z, N_X, N_CORE * ROWS, CHUNK)
    product = pl.pallas_call(
        project_kernel,
        grid_spec=pltpu.PrefetchScalarGridSpec(
            num_scalar_prefetch=1,
            grid=(1,),
            in_specs=[whole(a.shape) for a in operands],
            out_specs=whole(shape),
        ),
        out_shape=jax.ShapeDtypeStruct(shape, jnp.bfloat16),
        compiler_params=pltpu.CompilerParams(vmem_limit_bytes=BIG),
    )(jnp.stack([x, core]).astype(jnp.int32), *operands)
    summands = lax.all_to_all(
        product.reshape(N_EP, ROWS, CHUNK), "ep", split_axis=0, concat_axis=0, tiled=True
    )
    return summands.reshape(N_EP * ROWS, CHUNK)


def dispatch_kernel(summand_ref, residual_ref, gain_ref, pick_ref, attended_ref, out_ref):
    total = summand_ref[...].astype(jnp.float32).reshape(N_Z, N_PLANE * ROWS, CHUNK).sum(axis=0)
    columns = []
    for chunk in range(N_PLANE):
        source = chunk % N_X * N_CORE + chunk // N_X
        columns.append(total[source * ROWS : (source + 1) * ROWS])
    projected = jnp.concatenate(columns, axis=1)
    attended = (residual_ref[...].astype(jnp.float32) + projected).astype(jnp.bfloat16)
    attended_ref[...] = attended
    widened = attended.astype(jnp.float32)
    mean = jnp.sum(widened * widened, axis=1, keepdims=True) * (1.0 / D)
    normed = widened * lax.rsqrt(mean + NORM_EPSILON) * gain_ref[...].astype(jnp.float32)
    stacked = jnp.concatenate([normed[:, j * PART : (j + 1) * PART] for j in range(PARTS)], axis=0)
    out_ref[...] = jnp.dot(
        pick_ref[...], stacked.astype(jnp.bfloat16), preferred_element_type=jnp.float32
    ).astype(jnp.bfloat16)


def expert_kernel(layout, order_ref, *refs):
    count = len(layout)
    ins, (gate_ref, up_ref, down_ref) = refs[:count], refs[count : count + 3]
    outs = refs[count + 3 : 2 * count + 3]
    tokens, gate_sum, up_sum, hidden, results = refs[2 * count + 3 :]
    halves = [(i, h) for i, n in enumerate(layout) for h in range(n)]
    per_half = HALF // PARTS
    step = pl.program_id(0)

    @pl.when(step == 0)
    def _():
        for at, (i, h) in enumerate(halves):
            block = jnp.dot(
                order_ref[...], ins[i][h * HALF : (h + 1) * HALF, :], preferred_element_type=jnp.float32
            ).astype(jnp.bfloat16)
            for j in range(PARTS):
                tokens[j, at * per_half : (at + 1) * per_half, :] = block[j * per_half : (j + 1) * per_half]

    for i in range(STEPS):

        @pl.when(step == i)
        def _():
            gate = up = None
            for at in range(PER_STEP):
                part = tokens[i * PER_STEP + at]
                depth = slice(at * PART, (at + 1) * PART)
                more = jnp.dot(part, gate_ref[depth, :], preferred_element_type=jnp.float32)
                gate = more if gate is None else gate + more
                more = jnp.dot(part, up_ref[depth, :], preferred_element_type=jnp.float32)
                up = more if up is None else up + more
            if i > 0:
                gate, up = gate + gate_sum[...], up + up_sum[...]
            if i < STEPS - 1:
                gate_sum[...], up_sum[...] = gate, up
            else:
                hidden[...] = (gate * (1.0 / (1.0 + jnp.exp(-gate))) * up).astype(jnp.bfloat16)

        @pl.when(step == STEPS + i)
        def _():
            for at in range(PER_STEP):
                results[i * PER_STEP + at] = jnp.dot(
                    hidden[...], down_ref[:, at * PART : (at + 1) * PART], preferred_element_type=jnp.float32
                ).astype(jnp.bfloat16)

    @pl.when(step == 2 * STEPS - 1)
    def _():
        for at, (i, h) in enumerate(halves):
            block = jnp.concatenate(
                [results[j, at * per_half : (at + 1) * per_half, :] for j in range(PARTS)], axis=0
            )
            outs[i][h * HALF : (h + 1) * HALF, :] = lax.dot_general(
                order_ref[...], block, (((0,), (0,)), ((), ())), preferred_element_type=jnp.float32
            ).astype(jnp.bfloat16)


def expert(arrays, w_gate, w_up, w_down, order):
    layout = [a.shape[0] // HALF for a in arrays]
    rows = sum(layout) * HALF // PARTS
    span = PER_STEP * PART
    gate_spec = pl.BlockSpec((span, FF_PART), lambda i: (jnp.minimum(i, STEPS - 1), 0))
    down_spec = pl.BlockSpec((FF_PART, span), lambda i: (0, jnp.maximum(i - STEPS, 0)))
    return pl.pallas_call(
        functools.partial(expert_kernel, layout),
        grid=(2 * STEPS,),
        in_specs=[whole(order.shape)] + [whole(a.shape) for a in arrays] + [gate_spec, gate_spec, down_spec],
        out_specs=[whole(a.shape) for a in arrays],
        out_shape=[jax.ShapeDtypeStruct(a.shape, jnp.bfloat16) for a in arrays],
        scratch_shapes=[
            pltpu.VMEM((PARTS, rows, PART), jnp.bfloat16),
            pltpu.VMEM((rows, FF_PART), jnp.float32),
            pltpu.VMEM((rows, FF_PART), jnp.float32),
            pltpu.VMEM((rows, FF_PART), jnp.bfloat16),
            pltpu.VMEM((PARTS, rows, PART), jnp.bfloat16),
        ],
        compiler_params=pltpu.CompilerParams(vmem_limit_bytes=BIG),
        cost_estimate=pl.CostEstimate(
            flops=6 * rows * D * FF_PART, bytes_accessed=6 * D * FF_PART + 4 * rows * D, transcendentals=0
        ),
    )(order, *arrays, w_gate, w_up, w_down)


def finish_kernel(mix_ref, returned_ref, attended_ref, out_ref):
    summed = jnp.dot(mix_ref[...], returned_ref[...], preferred_element_type=jnp.float32)
    wide = PARTS * ROWS
    summed = summed[:wide] + summed[wide : 2 * wide] + summed[2 * wide :]
    mixture = jnp.concatenate([summed[j * ROWS : (j + 1) * ROWS] for j in range(PARTS)], axis=1)
    out_ref[...] = (attended_ref[...].astype(jnp.float32) + mixture).astype(jnp.bfloat16)


def routes(expert_ids, route_scores):
    shares = route_scores / jnp.sum(route_scores, axis=1, keepdims=True)
    named = expert_ids[:, :, None] == jnp.arange(N_EP)[None, None, :]
    hit = jnp.any(named, axis=1)
    share = jnp.sum(jnp.where(named, shares[:, :, None], 0.0), axis=1)
    row = jnp.arange(ROWS)
    earlier = row[None, :, None] < row[:, None, None]
    before = jnp.sum(jnp.where(earlier & hit[None], 1, 0), axis=1)
    slot = hit[:, :, None] & (before[:, :, None] == jnp.arange(CAP))
    same = jnp.arange(PARTS)[:, None] == jnp.arange(PARTS)[None, :]
    pick = jnp.where(
        slot.transpose(1, 2, 0)[:, None, :, None, :] & same[None, :, None, :, None], 1.0, 0.0
    ).reshape(N_EP * PARTS * CAP, PARTS * ROWS)
    mix = jnp.where(
        slot[None, :, :, None, :] & same[:, None, None, :, None], share[None, :, :, None, None], 0.0
    ).reshape(PARTS * ROWS, N_EP * PARTS * CAP)
    high = lax.reduce_precision(mix, 8, 7)
    middle = lax.reduce_precision(mix - high, 8, 7)
    low = mix - high - middle
    return pick.astype(jnp.bfloat16), jnp.concatenate([high, middle, low]).astype(jnp.bfloat16)


def order_matrix():
    half = N_EP // 2
    message = np.arange(HALF).reshape(half, PARTS, CAP)
    token = message.transpose(1, 0, 2).reshape(-1)
    return (token[:, None] == np.arange(HALF)[None, :]).astype(jnp.bfloat16)


def shards(
    residual,
    queries,
    token_keys,
    token_values,
    resident_cache,
    pool_block_cache,
    block_table,
    resumed,
    lengths,
    out_proj,
    norm_gain,
    expert_ids,
    route_scores,
    expert_gate,
    expert_up,
    expert_down,
):
    pool = lax.axis_index("pool")
    ep = lax.axis_index("ep")
    x, core = ep // N_CORE % N_X, ep % N_CORE

    blocks, facts, heads, asked = fetch_blocks(
        pool_block_cache[0], block_table, resumed, lengths, queries, pool
    )
    asked, out_proj = lax.optimization_barrier((asked, out_proj))
    cuts = cut_projection(pair_projection(out_proj, core), x)
    pick, mix = routes(expert_ids, route_scores)
    blocks[1], *cuts = lax.optimization_barrier((blocks[1], *cuts))
    pieces = [cuts[0]] + [shift_ep(cuts[d], x=d) for d in range(1, N_X)]
    context = attend(heads, token_keys, token_values, resident_cache, blocks, facts)
    context, *pieces = lax.optimization_barrier((context, *pieces))
    summands = project(context, pieces, x, core)
    message = (N_EP * PARTS * CAP, PART)
    attended, outgoing = pl.pallas_call(
        dispatch_kernel,
        out_shape=[
            jax.ShapeDtypeStruct((ROWS, D), jnp.bfloat16),
            jax.ShapeDtypeStruct(message, jnp.bfloat16),
        ],
        compiler_params=pltpu.CompilerParams(vmem_limit_bytes=BIG),
    )(summands, residual, norm_gain.reshape(1, D), pick)

    def exchange(rows):
        parted = rows.reshape(N_EP, PARTS * CAP, PART)
        return lax.all_to_all(parted, "ep", split_axis=0, concat_axis=0, tiled=True).reshape(message)

    weights = (expert_gate[0], expert_up[0], expert_down[0], jnp.asarray(order_matrix()))
    mine = exchange(outgoing)
    tie = lax.optimization_barrier

    def wide(value):
        return value.astype(jnp.float32)

    low, high = mine[:HALF], mine[HALF:]
    right_a, left_b = shift_pool(low, -1), shift_pool(high, 1)
    (own,) = expert([mine], *weights)
    right_a, left_b, own, low, high = tie((right_a, left_b, own, low, high))
    far_a, far_b = shift_pool(right_a, -1), shift_pool(left_b, 1)
    to_right_a, to_left_b = expert([right_a, left_b], *weights)
    low, high, to_right_a, to_left_b = tie((low, high, to_right_a, to_left_b))
    left_a, right_b = shift_pool(low, 1), shift_pool(high, -1)
    far_a, far_b, to_right_a, to_left_b = tie((far_a, far_b, to_right_a, to_left_b))
    to_far_a, to_far_b = expert([far_a, far_b], *weights)
    over_a, over_b = shift_pool(to_far_a, 1), shift_pool(to_far_b, -1)
    left_a, right_b, to_far_a, to_far_b = tie((left_a, right_b, to_far_a, to_far_b))
    to_left_a, to_right_b = expert([left_a, right_b], *weights)
    from_right_a, from_left_b = shift_pool(to_left_a, -1), shift_pool(to_right_b, 1)
    over_a, over_b, to_left_a = tie((over_a, over_b, to_left_a))
    from_left_a = shift_pool((wide(to_right_a) + wide(over_a)).astype(jnp.bfloat16), 1)
    from_right_b = shift_pool((wide(to_left_b) + wide(over_b)).astype(jnp.bfloat16), -1)
    base_a = wide(own[:HALF]) + wide(from_right_a)
    base_b = wide(own[HALF:]) + wide(from_left_b)
    summed = jnp.concatenate([base_a + wide(from_left_a), base_b + wide(from_right_b)]).astype(jnp.bfloat16)
    returned = exchange(summed)
    layer_out = pl.pallas_call(
        finish_kernel,
        out_shape=jax.ShapeDtypeStruct((ROWS, D), jnp.bfloat16),
        compiler_params=pltpu.CompilerParams(vmem_limit_bytes=BIG),
    )(mix, returned, attended)
    return (attended, layer_out)


def solution(mesh):
    placed = (
        P(("pool", "ep"), None),
        P(("pool", "ep"), None),
        P(("pool", "ep"), None),
        P(("pool", "ep"), None),
        P(("pool", "ep"), None, None, None),
        P("ep", "pool", None, None, None),
        P(("pool", "ep"), None),
        P(("pool", "ep")),
        P(("pool", "ep")),
        P("ep", None),
        P(),
        P(("pool", "ep"), None),
        P(("pool", "ep"), None),
        P("ep", None, "pool"),
        P("ep", None, "pool"),
        P("ep", "pool", None),
    )
    return jax.shard_map(
        shards,
        mesh=mesh,
        in_specs=placed,
        out_specs=(P(("pool", "ep"), None), P(("pool", "ep"), None)),
        check_vma=False,
    )
```

```python
import functools
import math

import jax
import jax.numpy as jnp
import numpy as np
from jax import lax
from jax.experimental import pallas as pl
from jax.experimental.pallas import tpu as pltpu
from jax.sharding import PartitionSpec as P

D = 4096
QUERY_HEADS = 64
KEY_VALUE_HEADS = 4
GROUP = QUERY_HEADS // KEY_VALUE_HEADS
HEAD_SIZE = 128
WIDE = KEY_VALUE_HEADS * HEAD_SIZE
CONTEXT_LIMIT = 64
BLOCK_POSITIONS = 16
RES_MOST = 4
CAP = 2
ROWS = 8
FACTS = 7
N_POOL = 4
N_Z, N_X, N_CORE = 8, 4, 2
N_PLANE = N_X * N_CORE
N_EP = N_Z * N_PLANE
DEEP = N_PLANE * HEAD_SIZE
CHUNK = D // N_PLANE
PARTS = 4
PART = D // PARTS
FF_PART = 384
STEPS = 2
PER_STEP = PARTS // STEPS
HALF = N_EP // 2 * PARTS * CAP
NORM_EPSILON = 1e-06
NEG_FILL = -1e30
BIG = 48 * 1024 * 1024
MOST = 60 * 1024 * 1024


def shift_pool(value, step):
    return lax.ppermute(value, "pool", [(i, (i + step) % N_POOL) for i in range(N_POOL)])


def shift_ep(value, x=0, core=0):
    pairs = []
    for i in range(N_EP):
        a, b, c = i // N_PLANE, i // N_CORE % N_X, i % N_CORE
        pairs.append((i, a * N_PLANE + (b + x) % N_X * N_CORE + (c + core) % N_CORE))
    return lax.ppermute(value, "ep", pairs)


def whole(shape):
    return pl.BlockSpec(shape, lambda *_: (0,) * len(shape))


def gather_kernel(asked_ref, cache_ref, *refs):
    outs, sems = refs[:N_POOL], refs[N_POOL]
    copies = []
    for d in range(N_POOL):
        for j in range(RES_MOST):
            copy = pltpu.make_async_copy(
                cache_ref.at[asked_ref[d * RES_MOST + j]], outs[d].at[j], sems.at[d * RES_MOST + j]
            )
            copy.start()
            copies.append(copy)
    for copy in copies:
        copy.wait()


def fetch_blocks(cache, block_table, resumed, lengths, queries, pool):
    slots = cache.shape[0]
    live = resumed > 0
    row = jnp.arange(ROWS)
    rank = jnp.sum(jnp.where(row[None, :] < row[:, None], resumed[None, :], 0), axis=1)
    rank = jnp.clip(rank, 0, RES_MOST - 1)
    holder = block_table // slots
    within = block_table % slots
    from_me = (pool + jnp.arange(N_POOL)) % N_POOL
    at_holder = holder[None] == from_me[:, None, None]
    at_rank = live[None, :] & (rank[None, :] == jnp.arange(RES_MOST)[:, None])
    chosen = at_holder[:, None] & at_rank[None, :, :, None]
    wanted = jnp.sum(jnp.where(chosen, within[None, None], 0), axis=(2, 3))
    start = jnp.arange(N_POOL) * BLOCK_POSITIONS
    place = jnp.sum(jnp.where(at_holder, start[None, None, :], 0), axis=2).T
    place = jnp.where(live[:, None], place, start[None, :])
    asked = jnp.concatenate([wanted[0]] + [shift_pool(wanted[d], d) for d in range(1, N_POOL)])
    asked = jnp.clip(asked, 0, slots - 1)
    facts = jnp.concatenate([rank[:, None], resumed[:, None], lengths[:, None], place], axis=1).reshape(-1)
    queries = queries.reshape(ROWS, QUERY_HEADS, HEAD_SIZE)
    shape = jax.ShapeDtypeStruct((RES_MOST,) + cache.shape[1:], jnp.bfloat16)
    gathered = pl.pallas_call(
        gather_kernel,
        grid_spec=pltpu.PrefetchScalarGridSpec(
            num_scalar_prefetch=1,
            grid=(1,),
            in_specs=[pl.BlockSpec(memory_space=pl.ANY)],
            out_specs=[whole((RES_MOST,) + cache.shape[1:])] * N_POOL,
            scratch_shapes=[pltpu.SemaphoreType.DMA((N_POOL * RES_MOST,))],
        ),
        out_shape=[shape] * N_POOL,
        cost_estimate=pl.CostEstimate(flops=0, bytes_accessed=1 << 20, transcendentals=0),
    )(asked, cache)
    blocks = [gathered[0]] + [shift_pool(gathered[d], -d) for d in range(1, N_POOL)]
    return blocks, facts, queries, asked


def attention_kernel(facts_ref, query_ref, key_ref, value_ref, resident_ref, b0, b1, b2, b3, out_ref):
    wider = CONTEXT_LIMIT + 16
    lane = lax.broadcasted_iota(jnp.int32, (1, wider), 1)
    head_of = lax.broadcasted_iota(jnp.int32, (QUERY_HEADS, WIDE), 0) // GROUP
    block_of = lax.broadcasted_iota(jnp.int32, (QUERY_HEADS, WIDE), 1) // HEAD_SIZE
    diagonal = head_of == block_of
    first = lax.broadcasted_iota(jnp.int32, (16, WIDE), 0) == 0
    factor = 1.0 / math.sqrt(HEAD_SIZE)
    results = []
    for row in range(ROWS):
        rank, resumed, length, *place = [facts_ref[row * FACTS + i] for i in range(FACTS)]
        is_resumed = resumed > 0

        def of_kind(kind, own_ref):
            loaded = jnp.concatenate([b[rank, kind] for b in (b0, b1, b2, b3)], axis=0)
            cached = jnp.where(is_resumed, loaded, resident_ref[row, kind])
            own = jnp.where(first, own_ref[row : row + 1, :].astype(jnp.float32), 0.0)
            return jnp.concatenate([cached, own.astype(jnp.bfloat16)], axis=0)

        keys, values = of_kind(0, key_ref), of_kind(1, value_ref)
        position = lane % BLOCK_POSITIONS
        for i in range(N_POOL):
            position = position + jnp.where(lane // BLOCK_POSITIONS == i, place[i], 0)
        live = ((lane < CONTEXT_LIMIT) & (position < length)) | (lane == CONTEXT_LIMIT)
        query = query_ref[row]
        query = jnp.where(diagonal, jnp.concatenate([query] * KEY_VALUE_HEADS, axis=1), 0)
        scores = lax.dot_general(
            query.astype(jnp.bfloat16), keys, (((1,), (1,)), ((), ())), preferred_element_type=jnp.float32
        )
        scores = jnp.where(live, scores * factor, NEG_FILL)
        highest = jnp.max(scores, axis=1, keepdims=True)
        raised = jnp.where(live, jnp.exp(scores - highest), 0.0)
        weights = (raised / jnp.sum(raised, axis=1, keepdims=True)).astype(jnp.bfloat16)
        spread = jnp.dot(weights, values, preferred_element_type=jnp.float32)
        results.append(
            jnp.concatenate(
                [
                    spread[k * GROUP : (k + 1) * GROUP, k * HEAD_SIZE : (k + 1) * HEAD_SIZE]
                    for k in range(KEY_VALUE_HEADS)
                ],
                axis=0,
            )
        )
    by_head = jnp.swapaxes(jnp.stack(results), 0, 1)
    planes = [
        jnp.concatenate([by_head[z * N_PLANE + h] for h in range(N_PLANE)], axis=1) for z in range(N_Z)
    ]
    out_ref[...] = jnp.concatenate(planes, axis=0).astype(jnp.bfloat16)


def attend(queries, token_keys, token_values, resident, blocks, facts):
    block = whole(blocks[0].shape)
    sent = N_Z * ROWS
    return pl.pallas_call(
        attention_kernel,
        grid_spec=pltpu.PrefetchScalarGridSpec(
            num_scalar_prefetch=1,
            grid=(1,),
            in_specs=[
                whole((ROWS, QUERY_HEADS, HEAD_SIZE)),
                whole((ROWS, WIDE)),
                whole((ROWS, WIDE)),
                whole(resident.shape),
                block,
                block,
                block,
                block,
            ],
            out_specs=whole((sent, DEEP)),
        ),
        out_shape=jax.ShapeDtypeStruct((sent, DEEP), jnp.bfloat16),
        compiler_params=pltpu.CompilerParams(vmem_limit_bytes=MOST),
        cost_estimate=pl.CostEstimate(flops=1 << 28, bytes_accessed=3 << 20, transcendentals=1 << 16),
    )(
        facts, queries, token_keys, token_values, resident, *blocks
    )


def pair_projection(out_proj, core):
    columns = N_X * CHUNK
    mine = lax.dynamic_slice_in_dim(out_proj, core * columns, columns, 1)
    other = lax.dynamic_slice_in_dim(out_proj, (1 - core) * columns, columns, 1)
    came = shift_ep(other, core=1)
    both = jnp.where(core == 0, jnp.stack([mine, came]), jnp.stack([came, mine]))
    return both.reshape(N_CORE * HEAD_SIZE, columns)


def cut_projection(pair, x):
    return [lax.dynamic_slice_in_dim(pair, (x + d) % N_X * CHUNK, CHUNK, 1) for d in range(N_X)]


def join_kernel(*refs):
    refs[-1][...] = jnp.concatenate([r[...] for r in refs[:-1]], axis=0)


def project_kernel(at_ref, mine_ref, other_ref, w0, w1, w2, w3, out_ref):
    x, core = at_ref[0], at_ref[1]
    width = N_CORE * HEAD_SIZE
    rows = N_Z * ROWS
    total = jnp.zeros((2 * N_X * rows, CHUNK), jnp.float32)
    for d, w_ref in enumerate((w0, w1, w2, w3)):
        source = (x + N_X - d) % N_X
        columns = pl.ds(pl.multiple_of(source * width, width), width)
        taken = jnp.concatenate([mine_ref[:, columns], other_ref[:, columns]], axis=0)
        total = total + jnp.dot(taken, w_ref[...], preferred_element_type=jnp.float32)
    for d in range(N_X):
        mine = total[d * rows : (d + 1) * rows].reshape(N_Z, ROWS, CHUNK)
        other = total[(N_X + d) * rows : (N_X + d + 1) * rows].reshape(N_Z, ROWS, CHUNK)
        first = jnp.where(core == 0, mine, other)
        second = jnp.where(core == 0, other, mine)
        both = jnp.concatenate([first, second], axis=1).astype(jnp.bfloat16)
        out_ref[:, pl.ds((x + N_X - d) % N_X, 1)] = both.reshape(N_Z, 1, N_CORE * ROWS, CHUNK)


def project(context, pieces, x, core):
    columns = [[z * N_PLANE + i for z in range(N_Z)] for i in range(N_PLANE)]
    local = lax.all_to_all(
        context.reshape(N_Z, ROWS, DEEP),
        "ep", split_axis=0, concat_axis=0, axis_index_groups=columns, tiled=True,
    ).reshape(N_Z * ROWS, DEEP)
    local, *pieces = lax.optimization_barrier((local, *pieces))
    far = [shift_ep(local, x=d) for d in range(1, N_X)]
    mine = pl.pallas_call(
        join_kernel,
        out_shape=jax.ShapeDtypeStruct((N_X * N_Z * ROWS, DEEP), jnp.bfloat16),
        compiler_params=pltpu.CompilerParams(vmem_limit_bytes=BIG),
    )(local, *far)
    operands = [mine, shift_ep(mine, core=1), *pieces]
    shape = (N_Z, N_X, N_CORE * ROWS, CHUNK)
    product = pl.pallas_call(
        project_kernel,
        grid_spec=pltpu.PrefetchScalarGridSpec(
            num_scalar_prefetch=1,
            grid=(1,),
            in_specs=[whole(a.shape) for a in operands],
            out_specs=whole(shape),
        ),
        out_shape=jax.ShapeDtypeStruct(shape, jnp.bfloat16),
        compiler_params=pltpu.CompilerParams(vmem_limit_bytes=BIG),
    )(jnp.stack([x, core]).astype(jnp.int32), *operands)
    summands = lax.all_to_all(
        product.reshape(N_EP, ROWS, CHUNK), "ep", split_axis=0, concat_axis=0, tiled=True
    )
    return summands.reshape(N_EP * ROWS, CHUNK)


def dispatch_kernel(summand_ref, residual_ref, gain_ref, pick_ref, attended_ref, out_ref):
    total = summand_ref[...].astype(jnp.float32).reshape(N_Z, N_PLANE * ROWS, CHUNK).sum(axis=0)
    columns = []
    for chunk in range(N_PLANE):
        source = chunk % N_X * N_CORE + chunk // N_X
        columns.append(total[source * ROWS : (source + 1) * ROWS])
    projected = jnp.concatenate(columns, axis=1)
    attended = (residual_ref[...].astype(jnp.float32) + projected).astype(jnp.bfloat16)
    attended_ref[...] = attended
    widened = attended.astype(jnp.float32)
    mean = jnp.sum(widened * widened, axis=1, keepdims=True) * (1.0 / D)
    normed = widened * lax.rsqrt(mean + NORM_EPSILON) * gain_ref[...].astype(jnp.float32)
    stacked = jnp.concatenate([normed[:, j * PART : (j + 1) * PART] for j in range(PARTS)], axis=0)
    out_ref[...] = jnp.dot(
        pick_ref[...], stacked.astype(jnp.bfloat16), preferred_element_type=jnp.float32
    ).astype(jnp.bfloat16)


def expert_kernel(layout, order_ref, *refs):
    count = len(layout)
    ins, (gate_ref, up_ref, down_ref) = refs[:count], refs[count : count + 3]
    outs = refs[count + 3 : 2 * count + 3]
    tokens, gate_sum, up_sum, hidden, results = refs[2 * count + 3 :]
    halves = [(i, h) for i, n in enumerate(layout) for h in range(n)]
    per_half = HALF // PARTS
    step = pl.program_id(0)

    @pl.when(step == 0)
    def _():
        for at, (i, h) in enumerate(halves):
            block = jnp.dot(
                order_ref[...], ins[i][h * HALF : (h + 1) * HALF, :], preferred_element_type=jnp.float32
            ).astype(jnp.bfloat16)
            for j in range(PARTS):
                tokens[j, at * per_half : (at + 1) * per_half, :] = block[j * per_half : (j + 1) * per_half]

    for i in range(STEPS):

        @pl.when(step == i)
        def _():
            gate = up = None
            for at in range(PER_STEP):
                part = tokens[i * PER_STEP + at]
                depth = slice(at * PART, (at + 1) * PART)
                more = jnp.dot(part, gate_ref[depth, :], preferred_element_type=jnp.float32)
                gate = more if gate is None else gate + more
                more = jnp.dot(part, up_ref[depth, :], preferred_element_type=jnp.float32)
                up = more if up is None else up + more
            if i > 0:
                gate, up = gate + gate_sum[...], up + up_sum[...]
            if i < STEPS - 1:
                gate_sum[...], up_sum[...] = gate, up
            else:
                hidden[...] = (gate * (1.0 / (1.0 + jnp.exp(-gate))) * up).astype(jnp.bfloat16)

        @pl.when(step == STEPS + i)
        def _():
            for at in range(PER_STEP):
                results[i * PER_STEP + at] = jnp.dot(
                    hidden[...], down_ref[:, at * PART : (at + 1) * PART], preferred_element_type=jnp.float32
                ).astype(jnp.bfloat16)

    @pl.when(step == 2 * STEPS - 1)
    def _():
        for at, (i, h) in enumerate(halves):
            block = jnp.concatenate(
                [results[j, at * per_half : (at + 1) * per_half, :] for j in range(PARTS)], axis=0
            )
            outs[i][h * HALF : (h + 1) * HALF, :] = lax.dot_general(
                order_ref[...], block, (((0,), (0,)), ((), ())), preferred_element_type=jnp.float32
            ).astype(jnp.bfloat16)


def expert(arrays, w_gate, w_up, w_down, order):
    layout = [a.shape[0] // HALF for a in arrays]
    rows = sum(layout) * HALF // PARTS
    span = PER_STEP * PART
    gate_spec = pl.BlockSpec((span, FF_PART), lambda i: (jnp.minimum(i, STEPS - 1), 0))
    down_spec = pl.BlockSpec((FF_PART, span), lambda i: (0, jnp.maximum(i - STEPS, 0)))
    return pl.pallas_call(
        functools.partial(expert_kernel, layout),
        grid=(2 * STEPS,),
        in_specs=[whole(order.shape)] + [whole(a.shape) for a in arrays] + [gate_spec, gate_spec, down_spec],
        out_specs=[whole(a.shape) for a in arrays],
        out_shape=[jax.ShapeDtypeStruct(a.shape, jnp.bfloat16) for a in arrays],
        scratch_shapes=[
            pltpu.VMEM((PARTS, rows, PART), jnp.bfloat16),
            pltpu.VMEM((rows, FF_PART), jnp.float32),
            pltpu.VMEM((rows, FF_PART), jnp.float32),
            pltpu.VMEM((rows, FF_PART), jnp.bfloat16),
            pltpu.VMEM((PARTS, rows, PART), jnp.bfloat16),
        ],
        compiler_params=pltpu.CompilerParams(vmem_limit_bytes=BIG),
        cost_estimate=pl.CostEstimate(
            flops=6 * rows * D * FF_PART, bytes_accessed=6 * D * FF_PART + 4 * rows * D, transcendentals=0
        ),
    )(order, *arrays, w_gate, w_up, w_down)


def finish_kernel(mix_ref, returned_ref, attended_ref, out_ref):
    summed = jnp.dot(mix_ref[...], returned_ref[...], preferred_element_type=jnp.float32)
    wide = PARTS * ROWS
    summed = summed[:wide] + summed[wide : 2 * wide] + summed[2 * wide :]
    mixture = jnp.concatenate([summed[j * ROWS : (j + 1) * ROWS] for j in range(PARTS)], axis=1)
    out_ref[...] = (attended_ref[...].astype(jnp.float32) + mixture).astype(jnp.bfloat16)


def routes(expert_ids, route_scores):
    shares = route_scores / jnp.sum(route_scores, axis=1, keepdims=True)
    named = expert_ids[:, :, None] == jnp.arange(N_EP)[None, None, :]
    hit = jnp.any(named, axis=1)
    share = jnp.sum(jnp.where(named, shares[:, :, None], 0.0), axis=1)
    row = jnp.arange(ROWS)
    earlier = row[None, :, None] < row[:, None, None]
    before = jnp.sum(jnp.where(earlier & hit[None], 1, 0), axis=1)
    slot = hit[:, :, None] & (before[:, :, None] == jnp.arange(CAP))
    same = jnp.arange(PARTS)[:, None] == jnp.arange(PARTS)[None, :]
    pick = jnp.where(
        slot.transpose(1, 2, 0)[:, None, :, None, :] & same[None, :, None, :, None], 1.0, 0.0
    ).reshape(N_EP * PARTS * CAP, PARTS * ROWS)
    mix = jnp.where(
        slot[None, :, :, None, :] & same[:, None, None, :, None], share[None, :, :, None, None], 0.0
    ).reshape(PARTS * ROWS, N_EP * PARTS * CAP)
    high = lax.reduce_precision(mix, 8, 7)
    middle = lax.reduce_precision(mix - high, 8, 7)
    low = mix - high - middle
    return pick.astype(jnp.bfloat16), jnp.concatenate([high, middle, low]).astype(jnp.bfloat16)


def order_matrix():
    half = N_EP // 2
    message = np.arange(HALF).reshape(half, PARTS, CAP)
    token = message.transpose(1, 0, 2).reshape(-1)
    return (token[:, None] == np.arange(HALF)[None, :]).astype(jnp.bfloat16)


def shards(
    residual,
    queries,
    token_keys,
    token_values,
    resident_cache,
    pool_block_cache,
    block_table,
    resumed,
    lengths,
    out_proj,
    norm_gain,
    expert_ids,
    route_scores,
    expert_gate,
    expert_up,
    expert_down,
):
    pool = lax.axis_index("pool")
    ep = lax.axis_index("ep")
    x, core = ep // N_CORE % N_X, ep % N_CORE

    blocks, facts, heads, asked = fetch_blocks(
        pool_block_cache[0], block_table, resumed, lengths, queries, pool
    )
    pair = pair_projection(out_proj, core)
    pick, mix = routes(expert_ids, route_scores)
    blocks[1], pair, facts, heads = lax.optimization_barrier((blocks[1], pair, facts, heads))
    cuts = cut_projection(pair, x)
    pieces = [cuts[0]] + [shift_ep(cuts[d], x=d) for d in range(1, N_X)]
    context = attend(heads, token_keys, token_values, resident_cache, blocks, facts)
    summands = project(context, pieces, x, core)
    message = (N_EP * PARTS * CAP, PART)
    attended, outgoing = pl.pallas_call(
        dispatch_kernel,
        out_shape=[
            jax.ShapeDtypeStruct((ROWS, D), jnp.bfloat16),
            jax.ShapeDtypeStruct(message, jnp.bfloat16),
        ],
        compiler_params=pltpu.CompilerParams(vmem_limit_bytes=BIG),
    )(summands, residual, norm_gain.reshape(1, D), pick)

    def exchange(rows):
        parted = rows.reshape(N_EP, PARTS * CAP, PART)
        return lax.all_to_all(parted, "ep", split_axis=0, concat_axis=0, tiled=True).reshape(message)

    weights = (expert_gate[0], expert_up[0], expert_down[0], jnp.asarray(order_matrix()))
    mine = exchange(outgoing)
    tie = lax.optimization_barrier

    def wide(value):
        return value.astype(jnp.float32)

    low, high = mine[:HALF], mine[HALF:]
    right_a, left_b = shift_pool(low, -1), shift_pool(high, 1)
    (own,) = expert([mine], *weights)
    right_a, left_b, own, low, high = tie((right_a, left_b, own, low, high))
    far_a, far_b = shift_pool(right_a, -1), shift_pool(left_b, 1)
    to_right_a, to_left_b = expert([right_a, left_b], *weights)
    low, high, to_right_a, to_left_b = tie((low, high, to_right_a, to_left_b))
    left_a, right_b = shift_pool(low, 1), shift_pool(high, -1)
    far_a, far_b, to_right_a, to_left_b = tie((far_a, far_b, to_right_a, to_left_b))
    to_far_a, to_far_b = expert([far_a, far_b], *weights)
    over_a, over_b = shift_pool(to_far_a, 1), shift_pool(to_far_b, -1)
    left_a, right_b, to_far_a, to_far_b = tie((left_a, right_b, to_far_a, to_far_b))
    to_left_a, to_right_b = expert([left_a, right_b], *weights)
    from_right_a, from_left_b = shift_pool(to_left_a, -1), shift_pool(to_right_b, 1)
    over_a, over_b, to_left_a = tie((over_a, over_b, to_left_a))
    from_left_a = shift_pool((wide(to_right_a) + wide(over_a)).astype(jnp.bfloat16), 1)
    from_right_b = shift_pool((wide(to_left_b) + wide(over_b)).astype(jnp.bfloat16), -1)
    base_a = wide(own[:HALF]) + wide(from_right_a)
    base_b = wide(own[HALF:]) + wide(from_left_b)
    summed = jnp.concatenate([base_a + wide(from_left_a), base_b + wide(from_right_b)]).astype(jnp.bfloat16)
    returned = exchange(summed)
    layer_out = pl.pallas_call(
        finish_kernel,
        out_shape=jax.ShapeDtypeStruct((ROWS, D), jnp.bfloat16),
        compiler_params=pltpu.CompilerParams(vmem_limit_bytes=BIG),
    )(mix, returned, attended)
    return (attended, layer_out)


def solution(mesh):
    placed = (
        P(("pool", "ep"), None),
        P(("pool", "ep"), None),
        P(("pool", "ep"), None),
        P(("pool", "ep"), None),
        P(("pool", "ep"), None, None, None),
        P("ep", "pool", None, None, None),
        P(("pool", "ep"), None),
        P(("pool", "ep")),
        P(("pool", "ep")),
        P("ep", None),
        P(),
        P(("pool", "ep"), None),
        P(("pool", "ep"), None),
        P("ep", None, "pool"),
        P("ep", None, "pool"),
        P("ep", "pool", None),
    )
    return jax.shard_map(
        shards,
        mesh=mesh,
        in_specs=placed,
        out_specs=(P(("pool", "ep"), None), P(("pool", "ep"), None)),
        check_vma=False,
    )
```

```python
import functools
import math

import jax
import jax.numpy as jnp
import numpy as np
from jax import lax
from jax.experimental import pallas as pl
from jax.experimental.pallas import tpu as pltpu
from jax.sharding import PartitionSpec as P

D = 4096
QUERY_HEADS = 64
KEY_VALUE_HEADS = 4
GROUP = QUERY_HEADS // KEY_VALUE_HEADS
HEAD_SIZE = 128
WIDE = KEY_VALUE_HEADS * HEAD_SIZE
CONTEXT_LIMIT = 64
BLOCK_POSITIONS = 16
RES_MOST = 4
CAP = 2
ROWS = 8
FACTS = 7
N_POOL = 4
N_Z, N_X, N_CORE = 8, 4, 2
N_PLANE = N_X * N_CORE
N_EP = N_Z * N_PLANE
DEEP = N_PLANE * HEAD_SIZE
CHUNK = D // N_PLANE
PARTS = 4
PART = D // PARTS
FF_PART = 384
STEPS = 2
PER_STEP = PARTS // STEPS
HALF = N_EP // 2 * PARTS * CAP
NORM_EPSILON = 1e-06
NEG_FILL = -1e30
BIG = 48 * 1024 * 1024
MOST = 60 * 1024 * 1024


def shift_pool(value, step):
    return lax.ppermute(value, "pool", [(i, (i + step) % N_POOL) for i in range(N_POOL)])


def shift_ep(value, x=0, core=0):
    pairs = []
    for i in range(N_EP):
        a, b, c = i // N_PLANE, i // N_CORE % N_X, i % N_CORE
        pairs.append((i, a * N_PLANE + (b + x) % N_X * N_CORE + (c + core) % N_CORE))
    return lax.ppermute(value, "ep", pairs)


def whole(shape):
    return pl.BlockSpec(shape, lambda *_: (0,) * len(shape))


def gather_kernel(*refs):
    asked, cache_ref = refs[:N_POOL], refs[N_POOL]
    outs, (slot_ref, sems) = refs[N_POOL + 1 : 2 * N_POOL + 1], refs[2 * N_POOL + 1 :]
    for i in range(N_POOL * RES_MOST):
        slot_ref[i] = 0
    for d in range(N_POOL):
        count = 0
        for row in range(ROWS):
            wanted = asked[d][row]
            at = d * RES_MOST + jnp.minimum(count, RES_MOST - 1)

            @pl.when(wanted >= 0)
            def _(wanted=wanted, at=at):
                slot_ref[at] = jnp.minimum(wanted, cache_ref.shape[0] - 1)

            count = count + jnp.where(wanted >= 0, 1, 0)
    copies = []
    for d in range(N_POOL):
        for j in range(RES_MOST):
            at = d * RES_MOST + j
            copy = pltpu.make_async_copy(cache_ref.at[slot_ref[at]], outs[d].at[j], sems.at[at])
            copy.start()
            copies.append(copy)
    for copy in copies:
        copy.wait()


def fetch_blocks(cache, block_table, resumed, lengths, queries, pool):
    slots = cache.shape[0]
    live = resumed > 0
    holder = block_table // slots
    within = block_table % slots
    from_me = (pool + jnp.arange(N_POOL)) % N_POOL
    at_holder = holder[None] == from_me[:, None, None]
    wanted = jnp.sum(jnp.where(at_holder, within[None], 0), axis=2)
    wanted = jnp.where(live[None, :], wanted, -1)
    asked = [wanted[0]] + [shift_pool(wanted[d], d) for d in range(1, N_POOL)]
    row = jnp.arange(ROWS)
    rank = jnp.sum(jnp.where(row[None, :] < row[:, None], resumed[None, :], 0), axis=1)
    rank = jnp.clip(rank, 0, RES_MOST - 1)
    start = jnp.arange(N_POOL) * BLOCK_POSITIONS
    place = jnp.sum(jnp.where(at_holder, start[None, None, :], 0), axis=2).T
    place = jnp.where(live[:, None], place, start[None, :])
    facts = jnp.concatenate([rank[:, None], resumed[:, None], lengths[:, None], place], axis=1).reshape(-1)
    queries = queries.reshape(ROWS, QUERY_HEADS, HEAD_SIZE)
    *asked, facts, queries = lax.optimization_barrier((*asked, facts, queries))
    shape = jax.ShapeDtypeStruct((RES_MOST,) + cache.shape[1:], jnp.bfloat16)
    gathered = pl.pallas_call(
        gather_kernel,
        grid_spec=pltpu.PrefetchScalarGridSpec(
            num_scalar_prefetch=N_POOL,
            grid=(1,),
            in_specs=[pl.BlockSpec(memory_space=pl.ANY)],
            out_specs=[whole(shape.shape)] * N_POOL,
            scratch_shapes=[
                pltpu.SMEM((N_POOL * RES_MOST,), jnp.int32),
                pltpu.SemaphoreType.DMA((N_POOL * RES_MOST,)),
            ],
        ),
        out_shape=[shape] * N_POOL,
        cost_estimate=pl.CostEstimate(flops=0, bytes_accessed=1 << 20, transcendentals=0),
    )(*asked, cache)
    blocks = [gathered[0]] + [shift_pool(gathered[d], -d) for d in range(1, N_POOL)]
    return blocks, facts, queries


def attention_kernel(facts_ref, query_ref, key_ref, value_ref, resident_ref, b0, b1, b2, b3, out_ref):
    wider = CONTEXT_LIMIT + 16
    lane = lax.broadcasted_iota(jnp.int32, (1, wider), 1)
    head_of = lax.broadcasted_iota(jnp.int32, (QUERY_HEADS, WIDE), 0) // GROUP
    block_of = lax.broadcasted_iota(jnp.int32, (QUERY_HEADS, WIDE), 1) // HEAD_SIZE
    diagonal = head_of == block_of
    first = lax.broadcasted_iota(jnp.int32, (16, WIDE), 0) == 0
    factor = 1.0 / math.sqrt(HEAD_SIZE)
    results = []
    for row in range(ROWS):
        rank, resumed, length, *place = [facts_ref[row * FACTS + i] for i in range(FACTS)]
        is_resumed = resumed > 0

        def of_kind(kind, own_ref):
            loaded = jnp.concatenate([b[rank, kind] for b in (b0, b1, b2, b3)], axis=0)
            cached = jnp.where(is_resumed, loaded, resident_ref[row, kind])
            own = jnp.where(first, own_ref[row : row + 1, :].astype(jnp.float32), 0.0)
            return jnp.concatenate([cached, own.astype(jnp.bfloat16)], axis=0)

        keys, values = of_kind(0, key_ref), of_kind(1, value_ref)
        position = lane % BLOCK_POSITIONS
        for i in range(N_POOL):
            position = position + jnp.where(lane // BLOCK_POSITIONS == i, place[i], 0)
        live = ((lane < CONTEXT_LIMIT) & (position < length)) | (lane == CONTEXT_LIMIT)
        query = query_ref[row]
        query = jnp.where(diagonal, jnp.concatenate([query] * KEY_VALUE_HEADS, axis=1), 0)
        scores = lax.dot_general(
            query.astype(jnp.bfloat16), keys, (((1,), (1,)), ((), ())), preferred_element_type=jnp.float32
        )
        scores = jnp.where(live, scores * factor, NEG_FILL)
        highest = jnp.max(scores, axis=1, keepdims=True)
        raised = jnp.where(live, jnp.exp(scores - highest), 0.0)
        weights = (raised / jnp.sum(raised, axis=1, keepdims=True)).astype(jnp.bfloat16)
        spread = jnp.dot(weights, values, preferred_element_type=jnp.float32)
        results.append(
            jnp.concatenate(
                [
                    spread[k * GROUP : (k + 1) * GROUP, k * HEAD_SIZE : (k + 1) * HEAD_SIZE]
                    for k in range(KEY_VALUE_HEADS)
                ],
                axis=0,
            )
        )
    by_head = jnp.swapaxes(jnp.stack(results), 0, 1)
    planes = [
        jnp.concatenate([by_head[z * N_PLANE + h] for h in range(N_PLANE)], axis=1) for z in range(N_Z)
    ]
    out_ref[...] = jnp.concatenate(planes, axis=0).astype(jnp.bfloat16)


def attend(queries, token_keys, token_values, resident, blocks, facts):
    block = whole(blocks[0].shape)
    sent = N_Z * ROWS
    return pl.pallas_call(
        attention_kernel,
        grid_spec=pltpu.PrefetchScalarGridSpec(
            num_scalar_prefetch=1,
            grid=(1,),
            in_specs=[
                whole((ROWS, QUERY_HEADS, HEAD_SIZE)),
                whole((ROWS, WIDE)),
                whole((ROWS, WIDE)),
                whole(resident.shape),
                block,
                block,
                block,
                block,
            ],
            out_specs=whole((sent, DEEP)),
        ),
        out_shape=jax.ShapeDtypeStruct((sent, DEEP), jnp.bfloat16),
        compiler_params=pltpu.CompilerParams(vmem_limit_bytes=MOST),
        cost_estimate=pl.CostEstimate(flops=1 << 28, bytes_accessed=3 << 20, transcendentals=1 << 16),
    )(
        facts, queries, token_keys, token_values, resident, *blocks
    )


def pair_projection(out_proj, core):
    columns = N_X * CHUNK
    mine = lax.dynamic_slice_in_dim(out_proj, core * columns, columns, 1)
    other = lax.dynamic_slice_in_dim(out_proj, (1 - core) * columns, columns, 1)
    came = shift_ep(other, core=1)
    both = jnp.where(core == 0, jnp.stack([mine, came]), jnp.stack([came, mine]))
    return both.reshape(N_CORE * HEAD_SIZE, columns)


def cut_projection(pair, x):
    return [lax.dynamic_slice_in_dim(pair, (x + d) % N_X * CHUNK, CHUNK, 1) for d in range(N_X)]


def join_kernel(*refs):
    refs[-1][...] = jnp.concatenate([r[...] for r in refs[:-1]], axis=0)


def project_kernel(at_ref, mine_ref, other_ref, w0, w1, w2, w3, out_ref):
    x, core = at_ref[0], at_ref[1]
    width = N_CORE * HEAD_SIZE
    rows = N_Z * ROWS
    total = jnp.zeros((2 * N_X * rows, CHUNK), jnp.float32)
    for d, w_ref in enumerate((w0, w1, w2, w3)):
        source = (x + N_X - d) % N_X
        columns = pl.ds(pl.multiple_of(source * width, width), width)
        taken = jnp.concatenate([mine_ref[:, columns], other_ref[:, columns]], axis=0)
        total = total + jnp.dot(taken, w_ref[...], preferred_element_type=jnp.float32)
    for d in range(N_X):
        mine = total[d * rows : (d + 1) * rows].reshape(N_Z, ROWS, CHUNK)
        other = total[(N_X + d) * rows : (N_X + d + 1) * rows].reshape(N_Z, ROWS, CHUNK)
        first = jnp.where(core == 0, mine, other)
        second = jnp.where(core == 0, other, mine)
        both = jnp.concatenate([first, second], axis=1).astype(jnp.bfloat16)
        out_ref[:, pl.ds((x + N_X - d) % N_X, 1)] = both.reshape(N_Z, 1, N_CORE * ROWS, CHUNK)


def project(context, pieces, x, core):
    columns = [[z * N_PLANE + i for z in range(N_Z)] for i in range(N_PLANE)]
    local = lax.all_to_all(
        context.reshape(N_Z, ROWS, DEEP),
        "ep", split_axis=0, concat_axis=0, axis_index_groups=columns, tiled=True,
    ).reshape(N_Z * ROWS, DEEP)
    local, *pieces = lax.optimization_barrier((local, *pieces))
    far = [shift_ep(local, x=d) for d in range(1, N_X)]
    mine = pl.pallas_call(
        join_kernel,
        out_shape=jax.ShapeDtypeStruct((N_X * N_Z * ROWS, DEEP), jnp.bfloat16),
        compiler_params=pltpu.CompilerParams(vmem_limit_bytes=BIG),
    )(local, *far)
    operands = [mine, shift_ep(mine, core=1), *pieces]
    shape = (N_Z, N_X, N_CORE * ROWS, CHUNK)
    product = pl.pallas_call(
        project_kernel,
        grid_spec=pltpu.PrefetchScalarGridSpec(
            num_scalar_prefetch=1,
            grid=(1,),
            in_specs=[whole(a.shape) for a in operands],
            out_specs=whole(shape),
        ),
        out_shape=jax.ShapeDtypeStruct(shape, jnp.bfloat16),
        compiler_params=pltpu.CompilerParams(vmem_limit_bytes=BIG),
    )(jnp.stack([x, core]).astype(jnp.int32), *operands)
    summands = lax.all_to_all(
        product.reshape(N_EP, ROWS, CHUNK), "ep", split_axis=0, concat_axis=0, tiled=True
    )
    return summands.reshape(N_EP * ROWS, CHUNK)


def dispatch_kernel(summand_ref, residual_ref, gain_ref, pick_ref, attended_ref, out_ref):
    total = summand_ref[...].astype(jnp.float32).reshape(N_Z, N_PLANE * ROWS, CHUNK).sum(axis=0)
    columns = []
    for chunk in range(N_PLANE):
        source = chunk % N_X * N_CORE + chunk // N_X
        columns.append(total[source * ROWS : (source + 1) * ROWS])
    projected = jnp.concatenate(columns, axis=1)
    attended = (residual_ref[...].astype(jnp.float32) + projected).astype(jnp.bfloat16)
    attended_ref[...] = attended
    widened = attended.astype(jnp.float32)
    mean = jnp.sum(widened * widened, axis=1, keepdims=True) * (1.0 / D)
    normed = widened * lax.rsqrt(mean + NORM_EPSILON) * gain_ref[...].astype(jnp.float32)
    stacked = jnp.concatenate([normed[:, j * PART : (j + 1) * PART] for j in range(PARTS)], axis=0)
    out_ref[...] = jnp.dot(
        pick_ref[...], stacked.astype(jnp.bfloat16), preferred_element_type=jnp.float32
    ).astype(jnp.bfloat16)


def expert_kernel(layout, order_ref, *refs):
    count = len(layout)
    ins, (gate_ref, up_ref, down_ref) = refs[:count], refs[count : count + 3]
    outs = refs[count + 3 : 2 * count + 3]
    tokens, gate_sum, up_sum, hidden, results = refs[2 * count + 3 :]
    halves = [(i, h) for i, n in enumerate(layout) for h in range(n)]
    per_half = HALF // PARTS
    step = pl.program_id(0)

    @pl.when(step == 0)
    def _():
        for at, (i, h) in enumerate(halves):
            block = jnp.dot(
                order_ref[...], ins[i][h * HALF : (h + 1) * HALF, :], preferred_element_type=jnp.float32
            ).astype(jnp.bfloat16)
            for j in range(PARTS):
                tokens[j, at * per_half : (at + 1) * per_half, :] = block[j * per_half : (j + 1) * per_half]

    @pl.when(step < STEPS)
    def _():
        gate = jnp.where(step == 0, 0.0, gate_sum[...])
        up = jnp.where(step == 0, 0.0, up_sum[...])
        for at in range(PER_STEP):
            part = tokens[jnp.minimum(step, STEPS - 1) * PER_STEP + at]
            depth = slice(at * PART, (at + 1) * PART)
            gate = gate + jnp.dot(part, gate_ref[depth, :], preferred_element_type=jnp.float32)
            up = up + jnp.dot(part, up_ref[depth, :], preferred_element_type=jnp.float32)
        gate_sum[...], up_sum[...] = gate, up

    @pl.when(step == STEPS)
    def _():
        gate = gate_sum[...]
        hidden[...] = (gate * (1.0 / (1.0 + jnp.exp(-gate))) * up_sum[...]).astype(jnp.bfloat16)

    @pl.when(step >= STEPS)
    def _():
        for at in range(PER_STEP):
            results[jnp.maximum(step - STEPS, 0) * PER_STEP + at] = jnp.dot(
                hidden[...], down_ref[:, at * PART : (at + 1) * PART], preferred_element_type=jnp.float32
            ).astype(jnp.bfloat16)

    @pl.when(step == 2 * STEPS - 1)
    def _():
        for at, (i, h) in enumerate(halves):
            block = jnp.concatenate(
                [results[j, at * per_half : (at + 1) * per_half, :] for j in range(PARTS)], axis=0
            )
            outs[i][h * HALF : (h + 1) * HALF, :] = lax.dot_general(
                order_ref[...], block, (((0,), (0,)), ((), ())), preferred_element_type=jnp.float32
            ).astype(jnp.bfloat16)


def expert(arrays, w_gate, w_up, w_down, order):
    layout = [a.shape[0] // HALF for a in arrays]
    rows = sum(layout) * HALF // PARTS
    span = PER_STEP * PART
    gate_spec = pl.BlockSpec((span, FF_PART), lambda i: (jnp.minimum(i, STEPS - 1), 0))
    down_spec = pl.BlockSpec((FF_PART, span), lambda i: (0, jnp.maximum(i - STEPS, 0)))
    return pl.pallas_call(
        functools.partial(expert_kernel, layout),
        grid=(2 * STEPS,),
        in_specs=[whole(order.shape)] + [whole(a.shape) for a in arrays] + [gate_spec, gate_spec, down_spec],
        out_specs=[whole(a.shape) for a in arrays],
        out_shape=[jax.ShapeDtypeStruct(a.shape, jnp.bfloat16) for a in arrays],
        scratch_shapes=[
            pltpu.VMEM((PARTS, rows, PART), jnp.bfloat16),
            pltpu.VMEM((rows, FF_PART), jnp.float32),
            pltpu.VMEM((rows, FF_PART), jnp.float32),
            pltpu.VMEM((rows, FF_PART), jnp.bfloat16),
            pltpu.VMEM((PARTS, rows, PART), jnp.bfloat16),
        ],
        compiler_params=pltpu.CompilerParams(vmem_limit_bytes=BIG),
        cost_estimate=pl.CostEstimate(
            flops=6 * rows * D * FF_PART, bytes_accessed=6 * D * FF_PART + 4 * rows * D, transcendentals=0
        ),
    )(order, *arrays, w_gate, w_up, w_down)


def sum_kernel(base_a_ref, base_b_ref, right_ref, left_ref, out_ref):
    out_ref[:HALF, :] = (base_a_ref[...] + right_ref[...].astype(jnp.float32)).astype(jnp.bfloat16)
    out_ref[HALF:, :] = (base_b_ref[...] + left_ref[...].astype(jnp.float32)).astype(jnp.bfloat16)


def finish_kernel(mix_ref, returned_ref, attended_ref, out_ref):
    summed = jnp.dot(mix_ref[...], returned_ref[...], preferred_element_type=jnp.float32)
    wide = PARTS * ROWS
    summed = summed[:wide] + summed[wide : 2 * wide] + summed[2 * wide :]
    mixture = jnp.concatenate([summed[j * ROWS : (j + 1) * ROWS] for j in range(PARTS)], axis=1)
    out_ref[...] = (attended_ref[...].astype(jnp.float32) + mixture).astype(jnp.bfloat16)


def routes(expert_ids, route_scores):
    shares = route_scores / jnp.sum(route_scores, axis=1, keepdims=True)
    named = expert_ids[:, :, None] == jnp.arange(N_EP)[None, None, :]
    hit = jnp.any(named, axis=1)
    share = jnp.sum(jnp.where(named, shares[:, :, None], 0.0), axis=1)
    row = jnp.arange(ROWS)
    earlier = row[None, :, None] < row[:, None, None]
    before = jnp.sum(jnp.where(earlier & hit[None], 1, 0), axis=1)
    slot = hit[:, :, None] & (before[:, :, None] == jnp.arange(CAP))
    same = jnp.arange(PARTS)[:, None] == jnp.arange(PARTS)[None, :]
    pick = jnp.where(
        slot.transpose(1, 2, 0)[:, None, :, None, :] & same[None, :, None, :, None], 1.0, 0.0
    ).reshape(N_EP * PARTS * CAP, PARTS * ROWS)
    mix = jnp.where(
        slot[None, :, :, None, :] & same[:, None, None, :, None], share[None, :, :, None, None], 0.0
    ).reshape(PARTS * ROWS, N_EP * PARTS * CAP)
    high = lax.reduce_precision(mix, 8, 7)
    middle = lax.reduce_precision(mix - high, 8, 7)
    low = mix - high - middle
    return pick.astype(jnp.bfloat16), jnp.concatenate([high, middle, low]).astype(jnp.bfloat16)


def order_matrix():
    half = N_EP // 2
    message = np.arange(HALF).reshape(half, PARTS, CAP)
    token = message.transpose(1, 0, 2).reshape(-1)
    return (token[:, None] == np.arange(HALF)[None, :]).astype(jnp.bfloat16)


def shards(
    residual,
    queries,
    token_keys,
    token_values,
    resident_cache,
    pool_block_cache,
    block_table,
    resumed,
    lengths,
    out_proj,
    norm_gain,
    expert_ids,
    route_scores,
    expert_gate,
    expert_up,
    expert_down,
):
    pool = lax.axis_index("pool")
    ep = lax.axis_index("ep")
    x, core = ep // N_CORE % N_X, ep % N_CORE

    blocks, facts, heads = fetch_blocks(
        pool_block_cache[0], block_table, resumed, lengths, queries, pool
    )
    pair = pair_projection(out_proj, core)
    pick, mix = routes(expert_ids, route_scores)
    blocks[1], pair, facts, heads = lax.optimization_barrier((blocks[1], pair, facts, heads))
    cuts = cut_projection(pair, x)
    pieces = [cuts[0]] + [shift_ep(cuts[d], x=d) for d in range(1, N_X)]
    context = attend(heads, token_keys, token_values, resident_cache, blocks, facts)
    summands = project(context, pieces, x, core)
    message = (N_EP * PARTS * CAP, PART)
    attended, outgoing = pl.pallas_call(
        dispatch_kernel,
        out_shape=[
            jax.ShapeDtypeStruct((ROWS, D), jnp.bfloat16),
            jax.ShapeDtypeStruct(message, jnp.bfloat16),
        ],
        compiler_params=pltpu.CompilerParams(vmem_limit_bytes=BIG),
    )(summands, residual, norm_gain.reshape(1, D), pick)

    def exchange(rows):
        parted = rows.reshape(N_EP, PARTS * CAP, PART)
        return lax.all_to_all(parted, "ep", split_axis=0, concat_axis=0, tiled=True).reshape(message)

    weights = (expert_gate[0], expert_up[0], expert_down[0], jnp.asarray(order_matrix()))
    mine = exchange(outgoing)
    left, right = shift_pool(mine, 1), shift_pool(mine, -1)
    (own,) = expert([mine], *weights)
    left, right, own = lax.optimization_barrier((left, right, own))
    far_a, far_b = shift_pool(right[:HALF], -1), shift_pool(left[HALF:], 1)
    to_left, to_right = expert([left, right], *weights)
    right_b, left_a = shift_pool(to_right[HALF:], 1), shift_pool(to_left[:HALF], -1)
    far_a, far_b, to_left, to_right = lax.optimization_barrier((far_a, far_b, to_left, to_right))
    to_far_a, to_far_b = expert([far_a, far_b], *weights)
    over_a, over_b = shift_pool(to_far_a, 1), shift_pool(to_far_b, -1)

    def wide(value):
        return value.astype(jnp.float32)

    base_a, base_b = wide(own[:HALF]) + wide(left_a), wide(own[HALF:]) + wide(right_b)
    over_a, over_b, base_a, base_b = lax.optimization_barrier((over_a, over_b, base_a, base_b))
    right_a = shift_pool((wide(to_right[:HALF]) + wide(over_a)).astype(jnp.bfloat16), 1)
    left_b = shift_pool((wide(to_left[HALF:]) + wide(over_b)).astype(jnp.bfloat16), -1)
    summed = pl.pallas_call(
        sum_kernel,
        out_shape=jax.ShapeDtypeStruct(message, jnp.bfloat16),
        compiler_params=pltpu.CompilerParams(vmem_limit_bytes=BIG),
    )(base_a, base_b, right_a, left_b)
    returned = exchange(summed)
    layer_out = pl.pallas_call(
        finish_kernel,
        out_shape=jax.ShapeDtypeStruct((ROWS, D), jnp.bfloat16),
        compiler_params=pltpu.CompilerParams(vmem_limit_bytes=BIG),
    )(mix, returned, attended)
    return (attended, layer_out)


def solution(mesh):
    placed = (
        P(("pool", "ep"), None),
        P(("pool", "ep"), None),
        P(("pool", "ep"), None),
        P(("pool", "ep"), None),
        P(("pool", "ep"), None, None, None),
        P("ep", "pool", None, None, None),
        P(("pool", "ep"), None),
        P(("pool", "ep")),
        P(("pool", "ep")),
        P("ep", None),
        P(),
        P(("pool", "ep"), None),
        P(("pool", "ep"), None),
        P("ep", None, "pool"),
        P("ep", None, "pool"),
        P("ep", "pool", None),
    )
    return jax.shard_map(
        shards,
        mesh=mesh,
        in_specs=placed,
        out_specs=(P(("pool", "ep"), None), P(("pool", "ep"), None)),
        check_vma=False,
    )
```

```python
import functools
import math

import jax
import jax.numpy as jnp
import numpy as np
from jax import lax
from jax.experimental import pallas as pl
from jax.experimental.pallas import tpu as pltpu
from jax.sharding import PartitionSpec as P

D = 4096
QUERY_HEADS = 64
KEY_VALUE_HEADS = 4
GROUP = QUERY_HEADS // KEY_VALUE_HEADS
HEAD_SIZE = 128
WIDE = KEY_VALUE_HEADS * HEAD_SIZE
CONTEXT_LIMIT = 64
BLOCK_POSITIONS = 16
RES_MOST = 4
CAP = 2
ROWS = 8
FACTS = 7
N_POOL = 4
N_Z, N_X, N_CORE = 8, 4, 2
N_PLANE = N_X * N_CORE
N_EP = N_Z * N_PLANE
DEEP = N_PLANE * HEAD_SIZE
CHUNK = D // N_PLANE
PARTS = 4
PART = D // PARTS
FF_PART = 384
STEPS = 2
PER_STEP = PARTS // STEPS
HALF = N_EP // 2 * PARTS * CAP
NORM_EPSILON = 1e-06
NEG_FILL = -1e30
BIG = 48 * 1024 * 1024
MOST = 60 * 1024 * 1024


def shift_pool(value, step):
    return lax.ppermute(value, "pool", [(i, (i + step) % N_POOL) for i in range(N_POOL)])


def shift_ep(value, x=0, core=0):
    pairs = []
    for i in range(N_EP):
        a, b, c = i // N_PLANE, i // N_CORE % N_X, i % N_CORE
        pairs.append((i, a * N_PLANE + (b + x) % N_X * N_CORE + (c + core) % N_CORE))
    return lax.ppermute(value, "ep", pairs)


def whole(shape):
    return pl.BlockSpec(shape, lambda *_: (0,) * len(shape))


def gather_kernel(*refs):
    asked, cache_ref = refs[:N_POOL], refs[N_POOL]
    outs, (slot_ref, sems) = refs[N_POOL + 1 : 2 * N_POOL + 1], refs[2 * N_POOL + 1 :]
    for i in range(N_POOL * RES_MOST):
        slot_ref[i] = 0
    for d in range(N_POOL):
        count = 0
        for row in range(ROWS):
            wanted = asked[d][row]
            at = d * RES_MOST + jnp.minimum(count, RES_MOST - 1)

            @pl.when(wanted >= 0)
            def _(wanted=wanted, at=at):
                slot_ref[at] = jnp.minimum(wanted, cache_ref.shape[0] - 1)

            count = count + jnp.where(wanted >= 0, 1, 0)
    copies = []
    for d in range(N_POOL):
        for j in range(RES_MOST):
            at = d * RES_MOST + j
            copy = pltpu.make_async_copy(cache_ref.at[slot_ref[at]], outs[d].at[j], sems.at[at])
            copy.start()
            copies.append(copy)
    for copy in copies:
        copy.wait()


def fetch_blocks(cache, block_table, resumed, lengths, queries, pool):
    slots = cache.shape[0]
    live = resumed > 0
    holder = block_table // slots
    within = block_table % slots
    from_me = (pool + jnp.arange(N_POOL)) % N_POOL
    at_holder = holder[None] == from_me[:, None, None]
    wanted = jnp.sum(jnp.where(at_holder, within[None], 0), axis=2)
    wanted = jnp.where(live[None, :], wanted, -1)
    asked = [wanted[0]] + [shift_pool(wanted[d], d) for d in range(1, N_POOL)]
    row = jnp.arange(ROWS)
    rank = jnp.sum(jnp.where(row[None, :] < row[:, None], resumed[None, :], 0), axis=1)
    rank = jnp.clip(rank, 0, RES_MOST - 1)
    start = jnp.arange(N_POOL) * BLOCK_POSITIONS
    place = jnp.sum(jnp.where(at_holder, start[None, None, :], 0), axis=2).T
    place = jnp.where(live[:, None], place, start[None, :])
    facts = jnp.concatenate([rank[:, None], resumed[:, None], lengths[:, None], place], axis=1).reshape(-1)
    queries = queries.reshape(ROWS, QUERY_HEADS, HEAD_SIZE)
    *asked, facts, queries = lax.optimization_barrier((*asked, facts, queries))
    shape = jax.ShapeDtypeStruct((RES_MOST,) + cache.shape[1:], jnp.bfloat16)
    gathered = pl.pallas_call(
        gather_kernel,
        grid_spec=pltpu.PrefetchScalarGridSpec(
            num_scalar_prefetch=N_POOL,
            grid=(1,),
            in_specs=[pl.BlockSpec(memory_space=pl.ANY)],
            out_specs=[whole(shape.shape)] * N_POOL,
            scratch_shapes=[
                pltpu.SMEM((N_POOL * RES_MOST,), jnp.int32),
                pltpu.SemaphoreType.DMA((N_POOL * RES_MOST,)),
            ],
        ),
        out_shape=[shape] * N_POOL,
        cost_estimate=pl.CostEstimate(flops=0, bytes_accessed=1 << 20, transcendentals=0),
    )(*asked, cache)
    blocks = [gathered[0]] + [shift_pool(gathered[d], -d) for d in range(1, N_POOL)]
    return blocks, facts, queries


def attention_kernel(facts_ref, query_ref, key_ref, value_ref, resident_ref, b0, b1, b2, b3, out_ref):
    wider = CONTEXT_LIMIT + 16
    lane = lax.broadcasted_iota(jnp.int32, (1, wider), 1)
    head_of = lax.broadcasted_iota(jnp.int32, (QUERY_HEADS, WIDE), 0) // GROUP
    block_of = lax.broadcasted_iota(jnp.int32, (QUERY_HEADS, WIDE), 1) // HEAD_SIZE
    diagonal = head_of == block_of
    first = lax.broadcasted_iota(jnp.int32, (16, WIDE), 0) == 0
    factor = 1.0 / math.sqrt(HEAD_SIZE)
    results = []
    for row in range(ROWS):
        rank, resumed, length, *place = [facts_ref[row * FACTS + i] for i in range(FACTS)]
        is_resumed = resumed > 0

        def of_kind(kind, own_ref):
            loaded = jnp.concatenate([b[rank, kind] for b in (b0, b1, b2, b3)], axis=0)
            cached = jnp.where(is_resumed, loaded, resident_ref[row, kind])
            own = jnp.where(first, own_ref[row : row + 1, :].astype(jnp.float32), 0.0)
            return jnp.concatenate([cached, own.astype(jnp.bfloat16)], axis=0)

        keys, values = of_kind(0, key_ref), of_kind(1, value_ref)
        position = lane % BLOCK_POSITIONS
        for i in range(N_POOL):
            position = position + jnp.where(lane // BLOCK_POSITIONS == i, place[i], 0)
        live = ((lane < CONTEXT_LIMIT) & (position < length)) | (lane == CONTEXT_LIMIT)
        query = query_ref[row]
        query = jnp.where(diagonal, jnp.concatenate([query] * KEY_VALUE_HEADS, axis=1), 0)
        scores = lax.dot_general(
            query.astype(jnp.bfloat16), keys, (((1,), (1,)), ((), ())), preferred_element_type=jnp.float32
        )
        scores = jnp.where(live, scores * factor, NEG_FILL)
        highest = jnp.max(scores, axis=1, keepdims=True)
        raised = jnp.where(live, jnp.exp(scores - highest), 0.0)
        weights = (raised / jnp.sum(raised, axis=1, keepdims=True)).astype(jnp.bfloat16)
        spread = jnp.dot(weights, values, preferred_element_type=jnp.float32)
        results.append(
            jnp.concatenate(
                [
                    spread[k * GROUP : (k + 1) * GROUP, k * HEAD_SIZE : (k + 1) * HEAD_SIZE]
                    for k in range(KEY_VALUE_HEADS)
                ],
                axis=0,
            )
        )
    by_head = jnp.swapaxes(jnp.stack(results), 0, 1)
    planes = [
        jnp.concatenate([by_head[z * N_PLANE + h] for h in range(N_PLANE)], axis=1) for z in range(N_Z)
    ]
    out_ref[...] = jnp.concatenate(planes, axis=0).astype(jnp.bfloat16)


def attend(queries, token_keys, token_values, resident, blocks, facts):
    block = whole(blocks[0].shape)
    sent = N_Z * ROWS
    return pl.pallas_call(
        attention_kernel,
        grid_spec=pltpu.PrefetchScalarGridSpec(
            num_scalar_prefetch=1,
            grid=(1,),
            in_specs=[
                whole((ROWS, QUERY_HEADS, HEAD_SIZE)),
                whole((ROWS, WIDE)),
                whole((ROWS, WIDE)),
                whole(resident.shape),
                block,
                block,
                block,
                block,
            ],
            out_specs=whole((sent, DEEP)),
        ),
        out_shape=jax.ShapeDtypeStruct((sent, DEEP), jnp.bfloat16),
        compiler_params=pltpu.CompilerParams(vmem_limit_bytes=MOST),
        cost_estimate=pl.CostEstimate(flops=1 << 28, bytes_accessed=3 << 20, transcendentals=1 << 16),
    )(
        facts, queries, token_keys, token_values, resident, *blocks
    )


def pair_projection(out_proj, core):
    columns = N_X * CHUNK
    mine = lax.dynamic_slice_in_dim(out_proj, core * columns, columns, 1)
    other = lax.dynamic_slice_in_dim(out_proj, (1 - core) * columns, columns, 1)
    came = shift_ep(other, core=1)
    both = jnp.where(core == 0, jnp.stack([mine, came]), jnp.stack([came, mine]))
    return both.reshape(N_CORE * HEAD_SIZE, columns)


def cut_projection(pair, x):
    return [lax.dynamic_slice_in_dim(pair, (x + d) % N_X * CHUNK, CHUNK, 1) for d in range(N_X)]


def join_kernel(*refs):
    refs[-1][...] = jnp.concatenate([r[...] for r in refs[:-1]], axis=0)


def project_kernel(at_ref, mine_ref, other_ref, w0, w1, w2, w3, out_ref):
    x, core = at_ref[0], at_ref[1]
    width = N_CORE * HEAD_SIZE
    rows = N_Z * ROWS
    total = jnp.zeros((2 * N_X * rows, CHUNK), jnp.float32)
    for d, w_ref in enumerate((w0, w1, w2, w3)):
        source = (x + N_X - d) % N_X
        columns = pl.ds(pl.multiple_of(source * width, width), width)
        taken = jnp.concatenate([mine_ref[:, columns], other_ref[:, columns]], axis=0)
        total = total + jnp.dot(taken, w_ref[...], preferred_element_type=jnp.float32)
    for d in range(N_X):
        mine = total[d * rows : (d + 1) * rows].reshape(N_Z, ROWS, CHUNK)
        other = total[(N_X + d) * rows : (N_X + d + 1) * rows].reshape(N_Z, ROWS, CHUNK)
        first = jnp.where(core == 0, mine, other)
        second = jnp.where(core == 0, other, mine)
        both = jnp.concatenate([first, second], axis=1).astype(jnp.bfloat16)
        out_ref[:, pl.ds((x + N_X - d) % N_X, 1)] = both.reshape(N_Z, 1, N_CORE * ROWS, CHUNK)


def project(context, pieces, x, core):
    columns = [[z * N_PLANE + i for z in range(N_Z)] for i in range(N_PLANE)]
    local = lax.all_to_all(
        context.reshape(N_Z, ROWS, DEEP),
        "ep", split_axis=0, concat_axis=0, axis_index_groups=columns, tiled=True,
    ).reshape(N_Z * ROWS, DEEP)
    local, *pieces = lax.optimization_barrier((local, *pieces))
    far = [shift_ep(local, x=d) for d in range(1, N_X)]
    mine = pl.pallas_call(
        join_kernel,
        out_shape=jax.ShapeDtypeStruct((N_X * N_Z * ROWS, DEEP), jnp.bfloat16),
        compiler_params=pltpu.CompilerParams(vmem_limit_bytes=BIG),
    )(local, *far)
    operands = [mine, shift_ep(mine, core=1), *pieces]
    shape = (N_Z, N_X, N_CORE * ROWS, CHUNK)
    product = pl.pallas_call(
        project_kernel,
        grid_spec=pltpu.PrefetchScalarGridSpec(
            num_scalar_prefetch=1,
            grid=(1,),
            in_specs=[whole(a.shape) for a in operands],
            out_specs=whole(shape),
        ),
        out_shape=jax.ShapeDtypeStruct(shape, jnp.bfloat16),
        compiler_params=pltpu.CompilerParams(vmem_limit_bytes=BIG),
    )(jnp.stack([x, core]).astype(jnp.int32), *operands)
    summands = lax.all_to_all(
        product.reshape(N_EP, ROWS, CHUNK), "ep", split_axis=0, concat_axis=0, tiled=True
    )
    return summands.reshape(N_EP * ROWS, CHUNK)


def dispatch_kernel(summand_ref, residual_ref, gain_ref, pick_ref, attended_ref, out_ref):
    total = summand_ref[...].astype(jnp.float32).reshape(N_Z, N_PLANE * ROWS, CHUNK).sum(axis=0)
    columns = []
    for chunk in range(N_PLANE):
        source = chunk % N_X * N_CORE + chunk // N_X
        columns.append(total[source * ROWS : (source + 1) * ROWS])
    projected = jnp.concatenate(columns, axis=1)
    attended = (residual_ref[...].astype(jnp.float32) + projected).astype(jnp.bfloat16)
    attended_ref[...] = attended
    widened = attended.astype(jnp.float32)
    mean = jnp.sum(widened * widened, axis=1, keepdims=True) * (1.0 / D)
    normed = widened * lax.rsqrt(mean + NORM_EPSILON) * gain_ref[...].astype(jnp.float32)
    stacked = jnp.concatenate([normed[:, j * PART : (j + 1) * PART] for j in range(PARTS)], axis=0)
    out_ref[...] = jnp.dot(
        pick_ref[...], stacked.astype(jnp.bfloat16), preferred_element_type=jnp.float32
    ).astype(jnp.bfloat16)


def expert_kernel(layout, order_ref, *refs):
    count = len(layout)
    ins, (gate_ref, up_ref, down_ref) = refs[:count], refs[count : count + 3]
    outs = refs[count + 3 : 2 * count + 3]
    tokens, gate_sum, up_sum, hidden, results = refs[2 * count + 3 :]
    halves = [(i, h) for i, n in enumerate(layout) for h in range(n)]
    per_half = HALF // PARTS
    step = pl.program_id(0)

    @pl.when(step == 0)
    def _():
        for at, (i, h) in enumerate(halves):
            block = jnp.dot(
                order_ref[...], ins[i][h * HALF : (h + 1) * HALF, :], preferred_element_type=jnp.float32
            ).astype(jnp.bfloat16)
            for j in range(PARTS):
                tokens[j, at * per_half : (at + 1) * per_half, :] = block[j * per_half : (j + 1) * per_half]

    @pl.when(step < STEPS)
    def _():
        gate = jnp.where(step == 0, 0.0, gate_sum[...])
        up = jnp.where(step == 0, 0.0, up_sum[...])
        for at in range(PER_STEP):
            part = tokens[jnp.minimum(step, STEPS - 1) * PER_STEP + at]
            depth = slice(at * PART, (at + 1) * PART)
            gate = gate + jnp.dot(part, gate_ref[depth, :], preferred_element_type=jnp.float32)
            up = up + jnp.dot(part, up_ref[depth, :], preferred_element_type=jnp.float32)
        gate_sum[...], up_sum[...] = gate, up

    @pl.when(step == STEPS)
    def _():
        gate = gate_sum[...]
        hidden[...] = (gate * (1.0 / (1.0 + jnp.exp(-gate))) * up_sum[...]).astype(jnp.bfloat16)

    @pl.when(step >= STEPS)
    def _():
        for at in range(PER_STEP):
            results[jnp.maximum(step - STEPS, 0) * PER_STEP + at] = jnp.dot(
                hidden[...], down_ref[:, at * PART : (at + 1) * PART], preferred_element_type=jnp.float32
            ).astype(jnp.bfloat16)

    @pl.when(step == 2 * STEPS - 1)
    def _():
        for at, (i, h) in enumerate(halves):
            block = jnp.concatenate(
                [results[j, at * per_half : (at + 1) * per_half, :] for j in range(PARTS)], axis=0
            )
            outs[i][h * HALF : (h + 1) * HALF, :] = lax.dot_general(
                order_ref[...], block, (((0,), (0,)), ((), ())), preferred_element_type=jnp.float32
            ).astype(jnp.bfloat16)


def expert(arrays, w_gate, w_up, w_down, order):
    layout = [a.shape[0] // HALF for a in arrays]
    rows = sum(layout) * HALF // PARTS
    span = PER_STEP * PART
    gate_spec = pl.BlockSpec((span, FF_PART), lambda i: (jnp.minimum(i, STEPS - 1), 0))
    down_spec = pl.BlockSpec((FF_PART, span), lambda i: (0, jnp.maximum(i - STEPS, 0)))
    return pl.pallas_call(
        functools.partial(expert_kernel, layout),
        grid=(2 * STEPS,),
        in_specs=[whole(order.shape)] + [whole(a.shape) for a in arrays] + [gate_spec, gate_spec, down_spec],
        out_specs=[whole(a.shape) for a in arrays],
        out_shape=[jax.ShapeDtypeStruct(a.shape, jnp.bfloat16) for a in arrays],
        scratch_shapes=[
            pltpu.VMEM((PARTS, rows, PART), jnp.bfloat16),
            pltpu.VMEM((rows, FF_PART), jnp.float32),
            pltpu.VMEM((rows, FF_PART), jnp.float32),
            pltpu.VMEM((rows, FF_PART), jnp.bfloat16),
            pltpu.VMEM((PARTS, rows, PART), jnp.bfloat16),
        ],
        compiler_params=pltpu.CompilerParams(vmem_limit_bytes=BIG),
        cost_estimate=pl.CostEstimate(
            flops=6 * rows * D * FF_PART, bytes_accessed=6 * D * FF_PART + 4 * rows * D, transcendentals=0
        ),
    )(order, *arrays, w_gate, w_up, w_down)


def sum_kernel(base_a_ref, base_b_ref, more_a_ref, more_b_ref, out_ref):
    out_ref[:HALF, :] = (base_a_ref[...] + more_a_ref[...].astype(jnp.float32)).astype(jnp.bfloat16)
    out_ref[HALF:, :] = (base_b_ref[...] + more_b_ref[...].astype(jnp.float32)).astype(jnp.bfloat16)


def finish_kernel(mix_ref, returned_ref, attended_ref, out_ref):
    summed = jnp.dot(mix_ref[...], returned_ref[...], preferred_element_type=jnp.float32)
    wide = PARTS * ROWS
    summed = summed[:wide] + summed[wide : 2 * wide] + summed[2 * wide :]
    mixture = jnp.concatenate([summed[j * ROWS : (j + 1) * ROWS] for j in range(PARTS)], axis=1)
    out_ref[...] = (attended_ref[...].astype(jnp.float32) + mixture).astype(jnp.bfloat16)


def routes(expert_ids, route_scores):
    shares = route_scores / jnp.sum(route_scores, axis=1, keepdims=True)
    named = expert_ids[:, :, None] == jnp.arange(N_EP)[None, None, :]
    hit = jnp.any(named, axis=1)
    share = jnp.sum(jnp.where(named, shares[:, :, None], 0.0), axis=1)
    row = jnp.arange(ROWS)
    earlier = row[None, :, None] < row[:, None, None]
    before = jnp.sum(jnp.where(earlier & hit[None], 1, 0), axis=1)
    slot = hit[:, :, None] & (before[:, :, None] == jnp.arange(CAP))
    same = jnp.arange(PARTS)[:, None] == jnp.arange(PARTS)[None, :]
    pick = jnp.where(
        slot.transpose(1, 2, 0)[:, None, :, None, :] & same[None, :, None, :, None], 1.0, 0.0
    ).reshape(N_EP * PARTS * CAP, PARTS * ROWS)
    mix = jnp.where(
        slot[None, :, :, None, :] & same[:, None, None, :, None], share[None, :, :, None, None], 0.0
    ).reshape(PARTS * ROWS, N_EP * PARTS * CAP)
    high = lax.reduce_precision(mix, 8, 7)
    middle = lax.reduce_precision(mix - high, 8, 7)
    low = mix - high - middle
    return pick.astype(jnp.bfloat16), jnp.concatenate([high, middle, low]).astype(jnp.bfloat16)


def order_matrix():
    half = N_EP // 2
    message = np.arange(HALF).reshape(half, PARTS, CAP)
    token = message.transpose(1, 0, 2).reshape(-1)
    return (token[:, None] == np.arange(HALF)[None, :]).astype(jnp.bfloat16)


def shards(
    residual,
    queries,
    token_keys,
    token_values,
    resident_cache,
    pool_block_cache,
    block_table,
    resumed,
    lengths,
    out_proj,
    norm_gain,
    expert_ids,
    route_scores,
    expert_gate,
    expert_up,
    expert_down,
):
    pool = lax.axis_index("pool")
    ep = lax.axis_index("ep")
    x, core = ep // N_CORE % N_X, ep % N_CORE

    blocks, facts, heads = fetch_blocks(
        pool_block_cache[0], block_table, resumed, lengths, queries, pool
    )
    pair = pair_projection(out_proj, core)
    pick, mix = routes(expert_ids, route_scores)
    blocks[1], pair, facts, heads = lax.optimization_barrier((blocks[1], pair, facts, heads))
    cuts = cut_projection(pair, x)
    pieces = [cuts[0]] + [shift_ep(cuts[d], x=d) for d in range(1, N_X)]
    context = attend(heads, token_keys, token_values, resident_cache, blocks, facts)
    summands = project(context, pieces, x, core)
    message = (N_EP * PARTS * CAP, PART)
    attended, outgoing = pl.pallas_call(
        dispatch_kernel,
        out_shape=[
            jax.ShapeDtypeStruct((ROWS, D), jnp.bfloat16),
            jax.ShapeDtypeStruct(message, jnp.bfloat16),
        ],
        compiler_params=pltpu.CompilerParams(vmem_limit_bytes=BIG),
    )(summands, residual, norm_gain.reshape(1, D), pick)

    def exchange(rows):
        parted = rows.reshape(N_EP, PARTS * CAP, PART)
        return lax.all_to_all(parted, "ep", split_axis=0, concat_axis=0, tiled=True).reshape(message)

    weights = (expert_gate[0], expert_up[0], expert_down[0], jnp.asarray(order_matrix()))
    mine = exchange(outgoing)
    tie = lax.optimization_barrier
    low, high = mine[:HALF], mine[HALF:]
    right_a, left_b = shift_pool(low, -1), shift_pool(high, 1)
    left_a, right_b = shift_pool(low, 1), shift_pool(high, -1)
    (own,) = expert([mine], *weights)
    right_a, left_b, own = tie((right_a, left_b, own))
    far_a, far_b = shift_pool(right_a, -1), shift_pool(left_b, 1)
    to_left_a, to_left_b, to_right_a, to_right_b = expert([left_a, left_b, right_a, right_b], *weights)
    from_left_b, from_right_a = shift_pool(to_right_b, 1), shift_pool(to_left_a, -1)
    far_a, far_b, to_left_b, to_right_a = tie((far_a, far_b, to_left_b, to_right_a))
    to_far_a, to_far_b = expert([far_a, far_b], *weights)
    over_a, over_b = shift_pool(to_far_a, 1), shift_pool(to_far_b, -1)

    def wide(value):
        return value.astype(jnp.float32)

    base_a, base_b = wide(own[:HALF]) + wide(from_right_a), wide(own[HALF:]) + wide(from_left_b)
    over_a, over_b, base_a, base_b = tie((over_a, over_b, base_a, base_b))
    from_left_a = shift_pool((wide(to_right_a) + wide(over_a)).astype(jnp.bfloat16), 1)
    from_right_b = shift_pool((wide(to_left_b) + wide(over_b)).astype(jnp.bfloat16), -1)
    summed = pl.pallas_call(
        sum_kernel,
        out_shape=jax.ShapeDtypeStruct(message, jnp.bfloat16),
        compiler_params=pltpu.CompilerParams(vmem_limit_bytes=BIG),
    )(base_a, base_b, from_left_a, from_right_b)
    returned = exchange(summed)
    layer_out = pl.pallas_call(
        finish_kernel,
        out_shape=jax.ShapeDtypeStruct((ROWS, D), jnp.bfloat16),
        compiler_params=pltpu.CompilerParams(vmem_limit_bytes=BIG),
    )(mix, returned, attended)
    return (attended, layer_out)


def solution(mesh):
    placed = (
        P(("pool", "ep"), None),
        P(("pool", "ep"), None),
        P(("pool", "ep"), None),
        P(("pool", "ep"), None),
        P(("pool", "ep"), None, None, None),
        P("ep", "pool", None, None, None),
        P(("pool", "ep"), None),
        P(("pool", "ep")),
        P(("pool", "ep")),
        P("ep", None),
        P(),
        P(("pool", "ep"), None),
        P(("pool", "ep"), None),
        P("ep", None, "pool"),
        P("ep", None, "pool"),
        P("ep", "pool", None),
    )
    return jax.shard_map(
        shards,
        mesh=mesh,
        in_specs=placed,
        out_specs=(P(("pool", "ep"), None), P(("pool", "ep"), None)),
        check_vma=False,
    )
```

```python
import functools
import math

import jax
import jax.numpy as jnp
import numpy as np
from jax import lax
from jax.experimental import pallas as pl
from jax.experimental.pallas import tpu as pltpu
from jax.sharding import PartitionSpec as P

D = 4096
QUERY_HEADS = 64
KEY_VALUE_HEADS = 4
GROUP = QUERY_HEADS // KEY_VALUE_HEADS
HEAD_SIZE = 128
WIDE = KEY_VALUE_HEADS * HEAD_SIZE
CONTEXT_LIMIT = 64
BLOCK_POSITIONS = 16
RES_MOST = 4
CAP = 2
ROWS = 8
FACTS = 7
N_POOL = 4
N_Z, N_X, N_CORE = 8, 4, 2
N_PLANE = N_X * N_CORE
N_EP = N_Z * N_PLANE
DEEP = N_PLANE * HEAD_SIZE
CHUNK = D // N_PLANE
PARTS = 4
PART = D // PARTS
FF_PART = 384
STEPS = 2
PER_STEP = PARTS // STEPS
HALF = N_EP // 2 * PARTS * CAP
NORM_EPSILON = 1e-06
NEG_FILL = -1e30
BIG = 48 * 1024 * 1024
MOST = 60 * 1024 * 1024


def shift_pool(value, step):
    return lax.ppermute(value, "pool", [(i, (i + step) % N_POOL) for i in range(N_POOL)])


def shift_ep(value, x=0, core=0):
    pairs = []
    for i in range(N_EP):
        a, b, c = i // N_PLANE, i // N_CORE % N_X, i % N_CORE
        pairs.append((i, a * N_PLANE + (b + x) % N_X * N_CORE + (c + core) % N_CORE))
    return lax.ppermute(value, "ep", pairs)


def whole(shape):
    return pl.BlockSpec(shape, lambda *_: (0,) * len(shape))


def gather_kernel(*refs):
    asked, cache_ref = refs[:N_POOL], refs[N_POOL]
    outs, (slot_ref, sems) = refs[N_POOL + 1 : 2 * N_POOL + 1], refs[2 * N_POOL + 1 :]
    for i in range(N_POOL * RES_MOST):
        slot_ref[i] = 0
    for d in range(N_POOL):
        count = 0
        for row in range(ROWS):
            wanted = asked[d][row]
            at = d * RES_MOST + jnp.minimum(count, RES_MOST - 1)

            @pl.when(wanted >= 0)
            def _(wanted=wanted, at=at):
                slot_ref[at] = jnp.minimum(wanted, cache_ref.shape[0] - 1)

            count = count + jnp.where(wanted >= 0, 1, 0)
    copies = []
    for d in range(N_POOL):
        for j in range(RES_MOST):
            at = d * RES_MOST + j
            copy = pltpu.make_async_copy(cache_ref.at[slot_ref[at]], outs[d].at[j], sems.at[at])
            copy.start()
            copies.append(copy)
    for copy in copies:
        copy.wait()


def fetch_blocks(cache, block_table, resumed, lengths, queries, pool):
    slots = cache.shape[0]
    live = resumed > 0
    holder = block_table // slots
    within = block_table % slots
    from_me = (pool + jnp.arange(N_POOL)) % N_POOL
    at_holder = holder[None] == from_me[:, None, None]
    wanted = jnp.sum(jnp.where(at_holder, within[None], 0), axis=2)
    wanted = jnp.where(live[None, :], wanted, -1)
    asked = [wanted[0]] + [shift_pool(wanted[d], d) for d in range(1, N_POOL)]
    row = jnp.arange(ROWS)
    rank = jnp.sum(jnp.where(row[None, :] < row[:, None], resumed[None, :], 0), axis=1)
    rank = jnp.clip(rank, 0, RES_MOST - 1)
    start = jnp.arange(N_POOL) * BLOCK_POSITIONS
    place = jnp.sum(jnp.where(at_holder, start[None, None, :], 0), axis=2).T
    place = jnp.where(live[:, None], place, start[None, :])
    facts = jnp.concatenate([rank[:, None], resumed[:, None], lengths[:, None], place], axis=1).reshape(-1)
    queries = queries.reshape(ROWS, QUERY_HEADS, HEAD_SIZE)
    *asked, facts, queries = lax.optimization_barrier((*asked, facts, queries))
    shape = jax.ShapeDtypeStruct((RES_MOST,) + cache.shape[1:], jnp.bfloat16)
    gathered = pl.pallas_call(
        gather_kernel,
        grid_spec=pltpu.PrefetchScalarGridSpec(
            num_scalar_prefetch=N_POOL,
            grid=(1,),
            in_specs=[pl.BlockSpec(memory_space=pl.ANY)],
            out_specs=[whole(shape.shape)] * N_POOL,
            scratch_shapes=[
                pltpu.SMEM((N_POOL * RES_MOST,), jnp.int32),
                pltpu.SemaphoreType.DMA((N_POOL * RES_MOST,)),
            ],
        ),
        out_shape=[shape] * N_POOL,
        cost_estimate=pl.CostEstimate(flops=0, bytes_accessed=1 << 20, transcendentals=0),
    )(*asked, cache)
    blocks = [gathered[0]] + [shift_pool(gathered[d], -d) for d in range(1, N_POOL)]
    return blocks, facts, queries


def attention_kernel(facts_ref, query_ref, key_ref, value_ref, resident_ref, b0, b1, b2, b3, out_ref):
    wider = CONTEXT_LIMIT + 16
    lane = lax.broadcasted_iota(jnp.int32, (1, wider), 1)
    head_of = lax.broadcasted_iota(jnp.int32, (QUERY_HEADS, WIDE), 0) // GROUP
    block_of = lax.broadcasted_iota(jnp.int32, (QUERY_HEADS, WIDE), 1) // HEAD_SIZE
    diagonal = head_of == block_of
    first = lax.broadcasted_iota(jnp.int32, (16, WIDE), 0) == 0
    factor = 1.0 / math.sqrt(HEAD_SIZE)
    results = []
    for row in range(ROWS):
        rank, resumed, length, *place = [facts_ref[row * FACTS + i] for i in range(FACTS)]
        is_resumed = resumed > 0

        def of_kind(kind, own_ref):
            loaded = jnp.concatenate([b[rank, kind] for b in (b0, b1, b2, b3)], axis=0)
            cached = jnp.where(is_resumed, loaded, resident_ref[row, kind])
            own = jnp.where(first, own_ref[row : row + 1, :].astype(jnp.float32), 0.0)
            return jnp.concatenate([cached, own.astype(jnp.bfloat16)], axis=0)

        keys, values = of_kind(0, key_ref), of_kind(1, value_ref)
        position = lane % BLOCK_POSITIONS
        for i in range(N_POOL):
            position = position + jnp.where(lane // BLOCK_POSITIONS == i, place[i], 0)
        live = ((lane < CONTEXT_LIMIT) & (position < length)) | (lane == CONTEXT_LIMIT)
        query = query_ref[row]
        query = jnp.where(diagonal, jnp.concatenate([query] * KEY_VALUE_HEADS, axis=1), 0)
        scores = lax.dot_general(
            query.astype(jnp.bfloat16), keys, (((1,), (1,)), ((), ())), preferred_element_type=jnp.float32
        )
        scores = jnp.where(live, scores * factor, NEG_FILL)
        highest = jnp.max(scores, axis=1, keepdims=True)
        raised = jnp.where(live, jnp.exp(scores - highest), 0.0)
        weights = (raised / jnp.sum(raised, axis=1, keepdims=True)).astype(jnp.bfloat16)
        spread = jnp.dot(weights, values, preferred_element_type=jnp.float32)
        results.append(
            jnp.concatenate(
                [
                    spread[k * GROUP : (k + 1) * GROUP, k * HEAD_SIZE : (k + 1) * HEAD_SIZE]
                    for k in range(KEY_VALUE_HEADS)
                ],
                axis=0,
            )
        )
    by_head = jnp.swapaxes(jnp.stack(results), 0, 1)
    planes = [
        jnp.concatenate([by_head[z * N_PLANE + h] for h in range(N_PLANE)], axis=1) for z in range(N_Z)
    ]
    out_ref[...] = jnp.concatenate(planes, axis=0).astype(jnp.bfloat16)


def attend(queries, token_keys, token_values, resident, blocks, facts):
    block = whole(blocks[0].shape)
    sent = N_Z * ROWS
    return pl.pallas_call(
        attention_kernel,
        grid_spec=pltpu.PrefetchScalarGridSpec(
            num_scalar_prefetch=1,
            grid=(1,),
            in_specs=[
                whole((ROWS, QUERY_HEADS, HEAD_SIZE)),
                whole((ROWS, WIDE)),
                whole((ROWS, WIDE)),
                whole(resident.shape),
                block,
                block,
                block,
                block,
            ],
            out_specs=whole((sent, DEEP)),
        ),
        out_shape=jax.ShapeDtypeStruct((sent, DEEP), jnp.bfloat16),
        compiler_params=pltpu.CompilerParams(vmem_limit_bytes=MOST),
        cost_estimate=pl.CostEstimate(flops=1 << 28, bytes_accessed=3 << 20, transcendentals=1 << 16),
    )(
        facts, queries, token_keys, token_values, resident, *blocks
    )


def pair_projection(out_proj, core):
    columns = N_X * CHUNK
    mine = lax.dynamic_slice_in_dim(out_proj, core * columns, columns, 1)
    other = lax.dynamic_slice_in_dim(out_proj, (1 - core) * columns, columns, 1)
    came = shift_ep(other, core=1)
    both = jnp.where(core == 0, jnp.stack([mine, came]), jnp.stack([came, mine]))
    return both.reshape(N_CORE * HEAD_SIZE, columns)


def cut_projection(pair, x):
    return [lax.dynamic_slice_in_dim(pair, (x + d) % N_X * CHUNK, CHUNK, 1) for d in range(N_X)]


def join_kernel(*refs):
    refs[-1][...] = jnp.concatenate([r[...] for r in refs[:-1]], axis=0)


def project_kernel(at_ref, mine_ref, other_ref, w0, w1, w2, w3, out_ref):
    x, core = at_ref[0], at_ref[1]
    width = N_CORE * HEAD_SIZE
    rows = N_Z * ROWS
    total = jnp.zeros((2 * N_X * rows, CHUNK), jnp.float32)
    for d, w_ref in enumerate((w0, w1, w2, w3)):
        source = (x + N_X - d) % N_X
        columns = pl.ds(pl.multiple_of(source * width, width), width)
        taken = jnp.concatenate([mine_ref[:, columns], other_ref[:, columns]], axis=0)
        total = total + jnp.dot(taken, w_ref[...], preferred_element_type=jnp.float32)
    for d in range(N_X):
        mine = total[d * rows : (d + 1) * rows].reshape(N_Z, ROWS, CHUNK)
        other = total[(N_X + d) * rows : (N_X + d + 1) * rows].reshape(N_Z, ROWS, CHUNK)
        first = jnp.where(core == 0, mine, other)
        second = jnp.where(core == 0, other, mine)
        both = jnp.concatenate([first, second], axis=1).astype(jnp.bfloat16)
        out_ref[:, pl.ds((x + N_X - d) % N_X, 1)] = both.reshape(N_Z, 1, N_CORE * ROWS, CHUNK)


def project(context, pieces, x, core):
    columns = [[z * N_PLANE + i for z in range(N_Z)] for i in range(N_PLANE)]
    local = lax.all_to_all(
        context.reshape(N_Z, ROWS, DEEP),
        "ep", split_axis=0, concat_axis=0, axis_index_groups=columns, tiled=True,
    ).reshape(N_Z * ROWS, DEEP)
    local, *pieces = lax.optimization_barrier((local, *pieces))
    far = [shift_ep(local, x=d) for d in range(1, N_X)]
    mine = pl.pallas_call(
        join_kernel,
        out_shape=jax.ShapeDtypeStruct((N_X * N_Z * ROWS, DEEP), jnp.bfloat16),
        compiler_params=pltpu.CompilerParams(vmem_limit_bytes=BIG),
    )(local, *far)
    operands = [mine, shift_ep(mine, core=1), *pieces]
    shape = (N_Z, N_X, N_CORE * ROWS, CHUNK)
    product = pl.pallas_call(
        project_kernel,
        grid_spec=pltpu.PrefetchScalarGridSpec(
            num_scalar_prefetch=1,
            grid=(1,),
            in_specs=[whole(a.shape) for a in operands],
            out_specs=whole(shape),
        ),
        out_shape=jax.ShapeDtypeStruct(shape, jnp.bfloat16),
        compiler_params=pltpu.CompilerParams(vmem_limit_bytes=BIG),
    )(jnp.stack([x, core]).astype(jnp.int32), *operands)
    summands = lax.all_to_all(
        product.reshape(N_EP, ROWS, CHUNK), "ep", split_axis=0, concat_axis=0, tiled=True
    )
    return summands.reshape(N_EP * ROWS, CHUNK)


def dispatch_kernel(summand_ref, residual_ref, gain_ref, pick_ref, attended_ref, out_ref):
    total = summand_ref[...].astype(jnp.float32).reshape(N_Z, N_PLANE * ROWS, CHUNK).sum(axis=0)
    columns = []
    for chunk in range(N_PLANE):
        source = chunk % N_X * N_CORE + chunk // N_X
        columns.append(total[source * ROWS : (source + 1) * ROWS])
    projected = jnp.concatenate(columns, axis=1)
    attended = (residual_ref[...].astype(jnp.float32) + projected).astype(jnp.bfloat16)
    attended_ref[...] = attended
    widened = attended.astype(jnp.float32)
    mean = jnp.sum(widened * widened, axis=1, keepdims=True) * (1.0 / D)
    normed = widened * lax.rsqrt(mean + NORM_EPSILON) * gain_ref[...].astype(jnp.float32)
    stacked = jnp.concatenate([normed[:, j * PART : (j + 1) * PART] for j in range(PARTS)], axis=0)
    out_ref[...] = jnp.dot(
        pick_ref[...], stacked.astype(jnp.bfloat16), preferred_element_type=jnp.float32
    ).astype(jnp.bfloat16)


def expert_kernel(layout, order_ref, *refs):
    count = len(layout)
    ins, (gate_ref, up_ref, down_ref) = refs[:count], refs[count : count + 3]
    outs = refs[count + 3 : 2 * count + 3]
    tokens, gate_sum, up_sum, hidden, results = refs[2 * count + 3 :]
    halves = [(i, h) for i, n in enumerate(layout) for h in range(n)]
    per_half = HALF // PARTS
    step = pl.program_id(0)

    @pl.when(step == 0)
    def _():
        for at, (i, h) in enumerate(halves):
            block = jnp.dot(
                order_ref[...], ins[i][h * HALF : (h + 1) * HALF, :], preferred_element_type=jnp.float32
            ).astype(jnp.bfloat16)
            for j in range(PARTS):
                tokens[j, at * per_half : (at + 1) * per_half, :] = block[j * per_half : (j + 1) * per_half]

    @pl.when(step < STEPS)
    def _():
        gate = jnp.where(step == 0, 0.0, gate_sum[...])
        up = jnp.where(step == 0, 0.0, up_sum[...])
        for at in range(PER_STEP):
            part = tokens[jnp.minimum(step, STEPS - 1) * PER_STEP + at]
            depth = slice(at * PART, (at + 1) * PART)
            gate = gate + jnp.dot(part, gate_ref[depth, :], preferred_element_type=jnp.float32)
            up = up + jnp.dot(part, up_ref[depth, :], preferred_element_type=jnp.float32)
        gate_sum[...], up_sum[...] = gate, up

    @pl.when(step == STEPS)
    def _():
        gate = gate_sum[...]
        hidden[...] = (gate * (1.0 / (1.0 + jnp.exp(-gate))) * up_sum[...]).astype(jnp.bfloat16)

    @pl.when(step >= STEPS)
    def _():
        for at in range(PER_STEP):
            results[jnp.maximum(step - STEPS, 0) * PER_STEP + at] = jnp.dot(
                hidden[...], down_ref[:, at * PART : (at + 1) * PART], preferred_element_type=jnp.float32
            ).astype(jnp.bfloat16)

    @pl.when(step == 2 * STEPS - 1)
    def _():
        for at, (i, h) in enumerate(halves):
            block = jnp.concatenate(
                [results[j, at * per_half : (at + 1) * per_half, :] for j in range(PARTS)], axis=0
            )
            outs[i][h * HALF : (h + 1) * HALF, :] = lax.dot_general(
                order_ref[...], block, (((0,), (0,)), ((), ())), preferred_element_type=jnp.float32
            ).astype(jnp.bfloat16)


def expert(arrays, w_gate, w_up, w_down, order, share=1):
    layout = [a.shape[0] // HALF for a in arrays]
    rows = sum(layout) * HALF // PARTS
    span = PER_STEP * PART
    gate_spec = pl.BlockSpec((span, FF_PART), lambda i: (jnp.minimum(i, STEPS - 1), 0))
    down_spec = pl.BlockSpec((FF_PART, span), lambda i: (0, jnp.maximum(i - STEPS, 0)))
    return pl.pallas_call(
        functools.partial(expert_kernel, layout),
        grid=(2 * STEPS,),
        in_specs=[whole(order.shape)] + [whole(a.shape) for a in arrays] + [gate_spec, gate_spec, down_spec],
        out_specs=[whole(a.shape) for a in arrays],
        out_shape=[jax.ShapeDtypeStruct(a.shape, jnp.bfloat16) for a in arrays],
        scratch_shapes=[
            pltpu.VMEM((PARTS, rows, PART), jnp.bfloat16),
            pltpu.VMEM((rows, FF_PART), jnp.float32),
            pltpu.VMEM((rows, FF_PART), jnp.float32),
            pltpu.VMEM((rows, FF_PART), jnp.bfloat16),
            pltpu.VMEM((PARTS, rows, PART), jnp.bfloat16),
        ],
        compiler_params=pltpu.CompilerParams(vmem_limit_bytes=BIG),
        cost_estimate=pl.CostEstimate(
            flops=6 * rows * D * FF_PART // share,
            bytes_accessed=(6 * D * FF_PART + 4 * rows * D) // share,
            transcendentals=0,
        ),
    )(order, *arrays, w_gate, w_up, w_down)


def sum_kernel(base_a_ref, base_b_ref, more_a_ref, more_b_ref, out_ref):
    out_ref[:HALF, :] = (base_a_ref[...] + more_a_ref[...].astype(jnp.float32)).astype(jnp.bfloat16)
    out_ref[HALF:, :] = (base_b_ref[...] + more_b_ref[...].astype(jnp.float32)).astype(jnp.bfloat16)


def finish_kernel(mix_ref, returned_ref, attended_ref, out_ref):
    summed = jnp.dot(mix_ref[...], returned_ref[...], preferred_element_type=jnp.float32)
    wide = PARTS * ROWS
    summed = summed[:wide] + summed[wide : 2 * wide] + summed[2 * wide :]
    mixture = jnp.concatenate([summed[j * ROWS : (j + 1) * ROWS] for j in range(PARTS)], axis=1)
    out_ref[...] = (attended_ref[...].astype(jnp.float32) + mixture).astype(jnp.bfloat16)


def routes(expert_ids, route_scores):
    shares = route_scores / jnp.sum(route_scores, axis=1, keepdims=True)
    named = expert_ids[:, :, None] == jnp.arange(N_EP)[None, None, :]
    hit = jnp.any(named, axis=1)
    share = jnp.sum(jnp.where(named, shares[:, :, None], 0.0), axis=1)
    row = jnp.arange(ROWS)
    earlier = row[None, :, None] < row[:, None, None]
    before = jnp.sum(jnp.where(earlier & hit[None], 1, 0), axis=1)
    slot = hit[:, :, None] & (before[:, :, None] == jnp.arange(CAP))
    same = jnp.arange(PARTS)[:, None] == jnp.arange(PARTS)[None, :]
    pick = jnp.where(
        slot.transpose(1, 2, 0)[:, None, :, None, :] & same[None, :, None, :, None], 1.0, 0.0
    ).reshape(N_EP * PARTS * CAP, PARTS * ROWS)
    mix = jnp.where(
        slot[None, :, :, None, :] & same[:, None, None, :, None], share[None, :, :, None, None], 0.0
    ).reshape(PARTS * ROWS, N_EP * PARTS * CAP)
    high = lax.reduce_precision(mix, 8, 7)
    middle = lax.reduce_precision(mix - high, 8, 7)
    low = mix - high - middle
    return pick.astype(jnp.bfloat16), jnp.concatenate([high, middle, low]).astype(jnp.bfloat16)


def order_matrix():
    half = N_EP // 2
    message = np.arange(HALF).reshape(half, PARTS, CAP)
    token = message.transpose(1, 0, 2).reshape(-1)
    return (token[:, None] == np.arange(HALF)[None, :]).astype(jnp.bfloat16)


def shards(
    residual,
    queries,
    token_keys,
    token_values,
    resident_cache,
    pool_block_cache,
    block_table,
    resumed,
    lengths,
    out_proj,
    norm_gain,
    expert_ids,
    route_scores,
    expert_gate,
    expert_up,
    expert_down,
):
    pool = lax.axis_index("pool")
    ep = lax.axis_index("ep")
    x, core = ep // N_CORE % N_X, ep % N_CORE

    blocks, facts, heads = fetch_blocks(
        pool_block_cache[0], block_table, resumed, lengths, queries, pool
    )
    pair = pair_projection(out_proj, core)
    pick, mix = routes(expert_ids, route_scores)
    blocks[1], pair, facts, heads = lax.optimization_barrier((blocks[1], pair, facts, heads))
    cuts = cut_projection(pair, x)
    pieces = [cuts[0]] + [shift_ep(cuts[d], x=d) for d in range(1, N_X)]
    context = attend(heads, token_keys, token_values, resident_cache, blocks, facts)
    summands = project(context, pieces, x, core)
    message = (N_EP * PARTS * CAP, PART)
    attended, outgoing = pl.pallas_call(
        dispatch_kernel,
        out_shape=[
            jax.ShapeDtypeStruct((ROWS, D), jnp.bfloat16),
            jax.ShapeDtypeStruct(message, jnp.bfloat16),
        ],
        compiler_params=pltpu.CompilerParams(vmem_limit_bytes=BIG),
    )(summands, residual, norm_gain.reshape(1, D), pick)

    def exchange(rows):
        parted = rows.reshape(N_EP, PARTS * CAP, PART)
        return lax.all_to_all(parted, "ep", split_axis=0, concat_axis=0, tiled=True).reshape(message)

    weights = (expert_gate[0], expert_up[0], expert_down[0], jnp.asarray(order_matrix()))
    mine = exchange(outgoing)
    tie = lax.optimization_barrier
    low, high = mine[:HALF], mine[HALF:]
    right_a, left_b = shift_pool(low, -1), shift_pool(high, 1)
    left_a, right_b = shift_pool(low, 1), shift_pool(high, -1)
    (own,) = expert([mine], *weights)
    right_a, left_b, own = tie((right_a, left_b, own))
    far_a, far_b = shift_pool(right_a, -1), shift_pool(left_b, 1)
    to_right_a, to_left_b = expert([right_a, left_b], *weights, share=64)
    from_left_a, from_right_b = shift_pool(to_right_a, 1), shift_pool(to_left_b, -1)
    far_a, far_b, left_a, right_b, to_right_a, to_left_b = tie(
        (far_a, far_b, left_a, right_b, to_right_a, to_left_b)
    )
    to_far_a, to_far_b = expert([far_a, far_b], *weights)
    over_a, over_b = shift_pool(to_far_a, -1), shift_pool(to_far_b, 1)
    left_a, right_b, to_far_a, to_far_b = tie((left_a, right_b, to_far_a, to_far_b))
    to_left_a, to_right_b = expert([left_a, right_b], *weights)

    def wide(value):
        return value.astype(jnp.float32)

    base_a, base_b = wide(own[:HALF]) + wide(from_left_a), wide(own[HALF:]) + wide(from_right_b)
    over_a, over_b, base_a, base_b = tie((over_a, over_b, base_a, base_b))
    from_right_a = shift_pool((wide(to_left_a) + wide(over_a)).astype(jnp.bfloat16), -1)
    from_left_b = shift_pool((wide(to_right_b) + wide(over_b)).astype(jnp.bfloat16), 1)
    summed = pl.pallas_call(
        sum_kernel,
        out_shape=jax.ShapeDtypeStruct(message, jnp.bfloat16),
        compiler_params=pltpu.CompilerParams(vmem_limit_bytes=BIG),
    )(base_a, base_b, from_right_a, from_left_b)
    returned = exchange(summed)
    layer_out = pl.pallas_call(
        finish_kernel,
        out_shape=jax.ShapeDtypeStruct((ROWS, D), jnp.bfloat16),
        compiler_params=pltpu.CompilerParams(vmem_limit_bytes=BIG),
    )(mix, returned, attended)
    return (attended, layer_out)


def solution(mesh):
    placed = (
        P(("pool", "ep"), None),
        P(("pool", "ep"), None),
        P(("pool", "ep"), None),
        P(("pool", "ep"), None),
        P(("pool", "ep"), None, None, None),
        P("ep", "pool", None, None, None),
        P(("pool", "ep"), None),
        P(("pool", "ep")),
        P(("pool", "ep")),
        P("ep", None),
        P(),
        P(("pool", "ep"), None),
        P(("pool", "ep"), None),
        P("ep", None, "pool"),
        P("ep", None, "pool"),
        P("ep", "pool", None),
    )
    return jax.shard_map(
        shards,
        mesh=mesh,
        in_specs=placed,
        out_specs=(P(("pool", "ep"), None), P(("pool", "ep"), None)),
        check_vma=False,
    )
```

```python
import functools
import math

import jax
import jax.numpy as jnp
import numpy as np
from jax import lax
from jax.experimental import pallas as pl
from jax.experimental.pallas import tpu as pltpu
from jax.sharding import PartitionSpec as P

D = 4096
QUERY_HEADS = 64
KEY_VALUE_HEADS = 4
GROUP = QUERY_HEADS // KEY_VALUE_HEADS
HEAD_SIZE = 128
WIDE = KEY_VALUE_HEADS * HEAD_SIZE
CONTEXT_LIMIT = 64
BLOCK_POSITIONS = 16
RES_MOST = 4
CAP = 2
ROWS = 8
FACTS = 7
N_POOL = 4
N_Z, N_X, N_CORE = 8, 4, 2
N_PLANE = N_X * N_CORE
N_EP = N_Z * N_PLANE
DEEP = N_PLANE * HEAD_SIZE
CHUNK = D // N_PLANE
PARTS = 4
PART = D // PARTS
FF_PART = 384
STEPS = 2
PER_STEP = PARTS // STEPS
HALF = N_EP // 2 * PARTS * CAP
NORM_EPSILON = 1e-06
NEG_FILL = -1e30
BIG = 48 * 1024 * 1024
MOST = 60 * 1024 * 1024


def shift_pool(value, step):
    return lax.ppermute(value, "pool", [(i, (i + step) % N_POOL) for i in range(N_POOL)])


def shift_ep(value, x=0, core=0):
    pairs = []
    for i in range(N_EP):
        a, b, c = i // N_PLANE, i // N_CORE % N_X, i % N_CORE
        pairs.append((i, a * N_PLANE + (b + x) % N_X * N_CORE + (c + core) % N_CORE))
    return lax.ppermute(value, "ep", pairs)


def whole(shape):
    return pl.BlockSpec(shape, lambda *_: (0,) * len(shape))


def gather_kernel(*refs):
    asked, cache_ref = refs[:N_POOL], refs[N_POOL]
    outs, (slot_ref, sems) = refs[N_POOL + 1 : 2 * N_POOL + 1], refs[2 * N_POOL + 1 :]
    for i in range(N_POOL * RES_MOST):
        slot_ref[i] = 0
    for d in range(N_POOL):
        count = 0
        for row in range(ROWS):
            wanted = asked[d][row]
            at = d * RES_MOST + jnp.minimum(count, RES_MOST - 1)

            @pl.when(wanted >= 0)
            def _(wanted=wanted, at=at):
                slot_ref[at] = jnp.minimum(wanted, cache_ref.shape[0] - 1)

            count = count + jnp.where(wanted >= 0, 1, 0)
    copies = []
    for d in range(N_POOL):
        for j in range(RES_MOST):
            at = d * RES_MOST + j
            copy = pltpu.make_async_copy(cache_ref.at[slot_ref[at]], outs[d].at[j], sems.at[at])
            copy.start()
            copies.append(copy)
    for copy in copies:
        copy.wait()


def fetch_blocks(cache, block_table, resumed, lengths, queries, pool):
    slots = cache.shape[0]
    live = resumed > 0
    holder = block_table // slots
    within = block_table % slots
    from_me = (pool + jnp.arange(N_POOL)) % N_POOL
    at_holder = holder[None] == from_me[:, None, None]
    wanted = jnp.sum(jnp.where(at_holder, within[None], 0), axis=2)
    wanted = jnp.where(live[None, :], wanted, -1)
    asked = [wanted[0]] + [shift_pool(wanted[d], d) for d in range(1, N_POOL)]
    row = jnp.arange(ROWS)
    rank = jnp.sum(jnp.where(row[None, :] < row[:, None], resumed[None, :], 0), axis=1)
    rank = jnp.clip(rank, 0, RES_MOST - 1)
    start = jnp.arange(N_POOL) * BLOCK_POSITIONS
    place = jnp.sum(jnp.where(at_holder, start[None, None, :], 0), axis=2).T
    place = jnp.where(live[:, None], place, start[None, :])
    facts = jnp.concatenate([rank[:, None], resumed[:, None], lengths[:, None], place], axis=1).reshape(-1)
    queries = queries.reshape(ROWS, QUERY_HEADS, HEAD_SIZE)
    *asked, facts, queries = lax.optimization_barrier((*asked, facts, queries))
    shape = jax.ShapeDtypeStruct((RES_MOST,) + cache.shape[1:], jnp.bfloat16)
    gathered = pl.pallas_call(
        gather_kernel,
        grid_spec=pltpu.PrefetchScalarGridSpec(
            num_scalar_prefetch=N_POOL,
            grid=(1,),
            in_specs=[pl.BlockSpec(memory_space=pl.ANY)],
            out_specs=[whole(shape.shape)] * N_POOL,
            scratch_shapes=[
                pltpu.SMEM((N_POOL * RES_MOST,), jnp.int32),
                pltpu.SemaphoreType.DMA((N_POOL * RES_MOST,)),
            ],
        ),
        out_shape=[shape] * N_POOL,
        cost_estimate=pl.CostEstimate(flops=0, bytes_accessed=1 << 20, transcendentals=0),
    )(*asked, cache)
    blocks = [gathered[0]] + [shift_pool(gathered[d], -d) for d in range(1, N_POOL)]
    return blocks, facts, queries


def attention_kernel(facts_ref, query_ref, key_ref, value_ref, resident_ref, b0, b1, b2, b3, out_ref):
    wider = CONTEXT_LIMIT + 16
    lane = lax.broadcasted_iota(jnp.int32, (1, wider), 1)
    head_of = lax.broadcasted_iota(jnp.int32, (QUERY_HEADS, WIDE), 0) // GROUP
    block_of = lax.broadcasted_iota(jnp.int32, (QUERY_HEADS, WIDE), 1) // HEAD_SIZE
    diagonal = head_of == block_of
    first = lax.broadcasted_iota(jnp.int32, (16, WIDE), 0) == 0
    factor = 1.0 / math.sqrt(HEAD_SIZE)
    results = []
    for row in range(ROWS):
        rank, resumed, length, *place = [facts_ref[row * FACTS + i] for i in range(FACTS)]
        is_resumed = resumed > 0

        def of_kind(kind, own_ref):
            loaded = jnp.concatenate([b[rank, kind] for b in (b0, b1, b2, b3)], axis=0)
            cached = jnp.where(is_resumed, loaded, resident_ref[row, kind])
            own = jnp.where(first, own_ref[row : row + 1, :].astype(jnp.float32), 0.0)
            return jnp.concatenate([cached, own.astype(jnp.bfloat16)], axis=0)

        keys, values = of_kind(0, key_ref), of_kind(1, value_ref)
        position = lane % BLOCK_POSITIONS
        for i in range(N_POOL):
            position = position + jnp.where(lane // BLOCK_POSITIONS == i, place[i], 0)
        live = ((lane < CONTEXT_LIMIT) & (position < length)) | (lane == CONTEXT_LIMIT)
        query = query_ref[row]
        query = jnp.where(diagonal, jnp.concatenate([query] * KEY_VALUE_HEADS, axis=1), 0)
        scores = lax.dot_general(
            query.astype(jnp.bfloat16), keys, (((1,), (1,)), ((), ())), preferred_element_type=jnp.float32
        )
        scores = jnp.where(live, scores * factor, NEG_FILL)
        highest = jnp.max(scores, axis=1, keepdims=True)
        raised = jnp.where(live, jnp.exp(scores - highest), 0.0)
        weights = (raised / jnp.sum(raised, axis=1, keepdims=True)).astype(jnp.bfloat16)
        spread = jnp.dot(weights, values, preferred_element_type=jnp.float32)
        results.append(
            jnp.concatenate(
                [
                    spread[k * GROUP : (k + 1) * GROUP, k * HEAD_SIZE : (k + 1) * HEAD_SIZE]
                    for k in range(KEY_VALUE_HEADS)
                ],
                axis=0,
            )
        )
    by_head = jnp.swapaxes(jnp.stack(results), 0, 1)
    planes = [
        jnp.concatenate([by_head[z * N_PLANE + h] for h in range(N_PLANE)], axis=1) for z in range(N_Z)
    ]
    out_ref[...] = jnp.concatenate(planes, axis=0).astype(jnp.bfloat16)


def attend(queries, token_keys, token_values, resident, blocks, facts):
    block = whole(blocks[0].shape)
    sent = N_Z * ROWS
    return pl.pallas_call(
        attention_kernel,
        grid_spec=pltpu.PrefetchScalarGridSpec(
            num_scalar_prefetch=1,
            grid=(1,),
            in_specs=[
                whole((ROWS, QUERY_HEADS, HEAD_SIZE)),
                whole((ROWS, WIDE)),
                whole((ROWS, WIDE)),
                whole(resident.shape),
                block,
                block,
                block,
                block,
            ],
            out_specs=whole((sent, DEEP)),
        ),
        out_shape=jax.ShapeDtypeStruct((sent, DEEP), jnp.bfloat16),
        compiler_params=pltpu.CompilerParams(vmem_limit_bytes=MOST),
        cost_estimate=pl.CostEstimate(flops=1 << 28, bytes_accessed=3 << 20, transcendentals=1 << 16),
    )(
        facts, queries, token_keys, token_values, resident, *blocks
    )


def pair_projection(out_proj, core):
    columns = N_X * CHUNK
    mine = lax.dynamic_slice_in_dim(out_proj, core * columns, columns, 1)
    other = lax.dynamic_slice_in_dim(out_proj, (1 - core) * columns, columns, 1)
    came = shift_ep(other, core=1)
    both = jnp.where(core == 0, jnp.stack([mine, came]), jnp.stack([came, mine]))
    return both.reshape(N_CORE * HEAD_SIZE, columns)


def cut_projection(pair, x):
    return [lax.dynamic_slice_in_dim(pair, (x + d) % N_X * CHUNK, CHUNK, 1) for d in range(N_X)]


def join_kernel(*refs):
    refs[-1][...] = jnp.concatenate([r[...] for r in refs[:-1]], axis=0)


def project_kernel(at_ref, mine_ref, other_ref, w0, w1, w2, w3, out_ref):
    x, core = at_ref[0], at_ref[1]
    width = N_CORE * HEAD_SIZE
    rows = N_Z * ROWS
    total = jnp.zeros((2 * N_X * rows, CHUNK), jnp.float32)
    for d, w_ref in enumerate((w0, w1, w2, w3)):
        source = (x + N_X - d) % N_X
        columns = pl.ds(pl.multiple_of(source * width, width), width)
        taken = jnp.concatenate([mine_ref[:, columns], other_ref[:, columns]], axis=0)
        total = total + jnp.dot(taken, w_ref[...], preferred_element_type=jnp.float32)
    for d in range(N_X):
        mine = total[d * rows : (d + 1) * rows].reshape(N_Z, ROWS, CHUNK)
        other = total[(N_X + d) * rows : (N_X + d + 1) * rows].reshape(N_Z, ROWS, CHUNK)
        first = jnp.where(core == 0, mine, other)
        second = jnp.where(core == 0, other, mine)
        both = jnp.concatenate([first, second], axis=1).astype(jnp.bfloat16)
        out_ref[:, pl.ds((x + N_X - d) % N_X, 1)] = both.reshape(N_Z, 1, N_CORE * ROWS, CHUNK)


def project(context, pieces, x, core):
    columns = [[z * N_PLANE + i for z in range(N_Z)] for i in range(N_PLANE)]
    local = lax.all_to_all(
        context.reshape(N_Z, ROWS, DEEP),
        "ep", split_axis=0, concat_axis=0, axis_index_groups=columns, tiled=True,
    ).reshape(N_Z * ROWS, DEEP)
    local, *pieces = lax.optimization_barrier((local, *pieces))
    far = [shift_ep(local, x=d) for d in range(1, N_X)]
    mine = pl.pallas_call(
        join_kernel,
        out_shape=jax.ShapeDtypeStruct((N_X * N_Z * ROWS, DEEP), jnp.bfloat16),
        compiler_params=pltpu.CompilerParams(vmem_limit_bytes=BIG),
    )(local, *far)
    operands = [mine, shift_ep(mine, core=1), *pieces]
    shape = (N_Z, N_X, N_CORE * ROWS, CHUNK)
    product = pl.pallas_call(
        project_kernel,
        grid_spec=pltpu.PrefetchScalarGridSpec(
            num_scalar_prefetch=1,
            grid=(1,),
            in_specs=[whole(a.shape) for a in operands],
            out_specs=whole(shape),
        ),
        out_shape=jax.ShapeDtypeStruct(shape, jnp.bfloat16),
        compiler_params=pltpu.CompilerParams(vmem_limit_bytes=BIG),
    )(jnp.stack([x, core]).astype(jnp.int32), *operands)
    summands = lax.all_to_all(
        product.reshape(N_EP, ROWS, CHUNK), "ep", split_axis=0, concat_axis=0, tiled=True
    )
    return summands.reshape(N_EP * ROWS, CHUNK)


def dispatch_kernel(summand_ref, residual_ref, gain_ref, pick_ref, attended_ref, out_ref):
    total = summand_ref[...].astype(jnp.float32).reshape(N_Z, N_PLANE * ROWS, CHUNK).sum(axis=0)
    columns = []
    for chunk in range(N_PLANE):
        source = chunk % N_X * N_CORE + chunk // N_X
        columns.append(total[source * ROWS : (source + 1) * ROWS])
    projected = jnp.concatenate(columns, axis=1)
    attended = (residual_ref[...].astype(jnp.float32) + projected).astype(jnp.bfloat16)
    attended_ref[...] = attended
    widened = attended.astype(jnp.float32)
    mean = jnp.sum(widened * widened, axis=1, keepdims=True) * (1.0 / D)
    normed = widened * lax.rsqrt(mean + NORM_EPSILON) * gain_ref[...].astype(jnp.float32)
    stacked = jnp.concatenate([normed[:, j * PART : (j + 1) * PART] for j in range(PARTS)], axis=0)
    out_ref[...] = jnp.dot(
        pick_ref[...], stacked.astype(jnp.bfloat16), preferred_element_type=jnp.float32
    ).astype(jnp.bfloat16)


def expert_kernel(layout, order_ref, *refs):
    count = len(layout)
    ins, (gate_ref, up_ref, down_ref) = refs[:count], refs[count : count + 3]
    outs = refs[count + 3 : 2 * count + 3]
    tokens, gate_sum, up_sum, hidden, results = refs[2 * count + 3 :]
    halves = [(i, h) for i, n in enumerate(layout) for h in range(n)]
    per_half = HALF // PARTS
    step = pl.program_id(0)

    @pl.when(step == 0)
    def _():
        for at, (i, h) in enumerate(halves):
            block = jnp.dot(
                order_ref[...], ins[i][h * HALF : (h + 1) * HALF, :], preferred_element_type=jnp.float32
            ).astype(jnp.bfloat16)
            for j in range(PARTS):
                tokens[j, at * per_half : (at + 1) * per_half, :] = block[j * per_half : (j + 1) * per_half]

    @pl.when(step < STEPS)
    def _():
        gate = jnp.where(step == 0, 0.0, gate_sum[...])
        up = jnp.where(step == 0, 0.0, up_sum[...])
        for at in range(PER_STEP):
            part = tokens[jnp.minimum(step, STEPS - 1) * PER_STEP + at]
            depth = slice(at * PART, (at + 1) * PART)
            gate = gate + jnp.dot(part, gate_ref[depth, :], preferred_element_type=jnp.float32)
            up = up + jnp.dot(part, up_ref[depth, :], preferred_element_type=jnp.float32)
        gate_sum[...], up_sum[...] = gate, up

    @pl.when(step == STEPS)
    def _():
        gate = gate_sum[...]
        hidden[...] = (gate * (1.0 / (1.0 + jnp.exp(-gate))) * up_sum[...]).astype(jnp.bfloat16)

    @pl.when(step >= STEPS)
    def _():
        for at in range(PER_STEP):
            results[jnp.maximum(step - STEPS, 0) * PER_STEP + at] = jnp.dot(
                hidden[...], down_ref[:, at * PART : (at + 1) * PART], preferred_element_type=jnp.float32
            ).astype(jnp.bfloat16)

    @pl.when(step == 2 * STEPS - 1)
    def _():
        for at, (i, h) in enumerate(halves):
            block = jnp.concatenate(
                [results[j, at * per_half : (at + 1) * per_half, :] for j in range(PARTS)], axis=0
            )
            outs[i][h * HALF : (h + 1) * HALF, :] = lax.dot_general(
                order_ref[...], block, (((0,), (0,)), ((), ())), preferred_element_type=jnp.float32
            ).astype(jnp.bfloat16)


def expert(arrays, w_gate, w_up, w_down, order, share=1):
    layout = [a.shape[0] // HALF for a in arrays]
    rows = sum(layout) * HALF // PARTS
    span = PER_STEP * PART
    gate_spec = pl.BlockSpec((span, FF_PART), lambda i: (jnp.minimum(i, STEPS - 1), 0))
    down_spec = pl.BlockSpec((FF_PART, span), lambda i: (0, jnp.maximum(i - STEPS, 0)))
    return pl.pallas_call(
        functools.partial(expert_kernel, layout),
        grid=(2 * STEPS,),
        in_specs=[whole(order.shape)] + [whole(a.shape) for a in arrays] + [gate_spec, gate_spec, down_spec],
        out_specs=[whole(a.shape) for a in arrays],
        out_shape=[jax.ShapeDtypeStruct(a.shape, jnp.bfloat16) for a in arrays],
        scratch_shapes=[
            pltpu.VMEM((PARTS, rows, PART), jnp.bfloat16),
            pltpu.VMEM((rows, FF_PART), jnp.float32),
            pltpu.VMEM((rows, FF_PART), jnp.float32),
            pltpu.VMEM((rows, FF_PART), jnp.bfloat16),
            pltpu.VMEM((PARTS, rows, PART), jnp.bfloat16),
        ],
        compiler_params=pltpu.CompilerParams(vmem_limit_bytes=BIG),
        cost_estimate=pl.CostEstimate(
            flops=6 * rows * D * FF_PART // share,
            bytes_accessed=(6 * D * FF_PART + 4 * rows * D) // share,
            transcendentals=0,
        ),
    )(order, *arrays, w_gate, w_up, w_down)


def sum_kernel(base_a_ref, base_b_ref, more_a_ref, more_b_ref, out_ref):
    out_ref[:HALF, :] = (base_a_ref[...] + more_a_ref[...].astype(jnp.float32)).astype(jnp.bfloat16)
    out_ref[HALF:, :] = (base_b_ref[...] + more_b_ref[...].astype(jnp.float32)).astype(jnp.bfloat16)


def finish_kernel(mix_ref, returned_ref, attended_ref, out_ref):
    summed = jnp.dot(mix_ref[...], returned_ref[...], preferred_element_type=jnp.float32)
    wide = PARTS * ROWS
    summed = summed[:wide] + summed[wide : 2 * wide] + summed[2 * wide :]
    mixture = jnp.concatenate([summed[j * ROWS : (j + 1) * ROWS] for j in range(PARTS)], axis=1)
    out_ref[...] = (attended_ref[...].astype(jnp.float32) + mixture).astype(jnp.bfloat16)


def routes(expert_ids, route_scores):
    shares = route_scores / jnp.sum(route_scores, axis=1, keepdims=True)
    named = expert_ids[:, :, None] == jnp.arange(N_EP)[None, None, :]
    hit = jnp.any(named, axis=1)
    share = jnp.sum(jnp.where(named, shares[:, :, None], 0.0), axis=1)
    row = jnp.arange(ROWS)
    earlier = row[None, :, None] < row[:, None, None]
    before = jnp.sum(jnp.where(earlier & hit[None], 1, 0), axis=1)
    slot = hit[:, :, None] & (before[:, :, None] == jnp.arange(CAP))
    same = jnp.arange(PARTS)[:, None] == jnp.arange(PARTS)[None, :]
    pick = jnp.where(
        slot.transpose(1, 2, 0)[:, None, :, None, :] & same[None, :, None, :, None], 1.0, 0.0
    ).reshape(N_EP * PARTS * CAP, PARTS * ROWS)
    mix = jnp.where(
        slot[None, :, :, None, :] & same[:, None, None, :, None], share[None, :, :, None, None], 0.0
    ).reshape(PARTS * ROWS, N_EP * PARTS * CAP)
    high = lax.reduce_precision(mix, 8, 7)
    middle = lax.reduce_precision(mix - high, 8, 7)
    low = mix - high - middle
    return pick.astype(jnp.bfloat16), jnp.concatenate([high, middle, low]).astype(jnp.bfloat16)


def order_matrix():
    half = N_EP // 2
    message = np.arange(HALF).reshape(half, PARTS, CAP)
    token = message.transpose(1, 0, 2).reshape(-1)
    return (token[:, None] == np.arange(HALF)[None, :]).astype(jnp.bfloat16)


def shards(
    residual,
    queries,
    token_keys,
    token_values,
    resident_cache,
    pool_block_cache,
    block_table,
    resumed,
    lengths,
    out_proj,
    norm_gain,
    expert_ids,
    route_scores,
    expert_gate,
    expert_up,
    expert_down,
):
    pool = lax.axis_index("pool")
    ep = lax.axis_index("ep")
    x, core = ep // N_CORE % N_X, ep % N_CORE

    blocks, facts, heads = fetch_blocks(
        pool_block_cache[0], block_table, resumed, lengths, queries, pool
    )
    pair = pair_projection(out_proj, core)
    pick, mix = routes(expert_ids, route_scores)
    blocks[1], pair, facts, heads = lax.optimization_barrier((blocks[1], pair, facts, heads))
    cuts = cut_projection(pair, x)
    pieces = [cuts[0]] + [shift_ep(cuts[d], x=d) for d in range(1, N_X)]
    context = attend(heads, token_keys, token_values, resident_cache, blocks, facts)
    summands = project(context, pieces, x, core)
    message = (N_EP * PARTS * CAP, PART)
    attended, outgoing = pl.pallas_call(
        dispatch_kernel,
        out_shape=[
            jax.ShapeDtypeStruct((ROWS, D), jnp.bfloat16),
            jax.ShapeDtypeStruct(message, jnp.bfloat16),
        ],
        compiler_params=pltpu.CompilerParams(vmem_limit_bytes=BIG),
    )(summands, residual, norm_gain.reshape(1, D), pick)

    def exchange(rows):
        parted = rows.reshape(N_EP, PARTS * CAP, PART)
        return lax.all_to_all(parted, "ep", split_axis=0, concat_axis=0, tiled=True).reshape(message)

    weights = (expert_gate[0], expert_up[0], expert_down[0], jnp.asarray(order_matrix()))
    mine = exchange(outgoing)
    tie = lax.optimization_barrier
    low, high = mine[:HALF], mine[HALF:]
    right_a, left_b = shift_pool(low, -1), shift_pool(high, 1)
    left_a, right_b = shift_pool(low, 1), shift_pool(high, -1)
    (own,) = expert([mine], *weights)
    right_a, left_b, own = tie((right_a, left_b, own))
    far_a, far_b = shift_pool(right_a, -1), shift_pool(left_b, 1)
    to_right_a, to_left_b = expert([right_a, left_b], *weights, share=64)
    far_a, far_b, left_a, right_b, to_right_a, to_left_b = tie(
        (far_a, far_b, left_a, right_b, to_right_a, to_left_b)
    )
    from_left_a, from_right_b = shift_pool(to_right_a, 1), shift_pool(to_left_b, -1)
    to_far_a, to_far_b = expert([far_a, far_b], *weights)
    over_a, over_b = shift_pool(to_far_a, -1), shift_pool(to_far_b, 1)
    left_a, right_b, to_far_a, to_far_b = tie((left_a, right_b, to_far_a, to_far_b))
    to_left_a, to_right_b = expert([left_a, right_b], *weights)

    def wide(value):
        return value.astype(jnp.float32)

    base_a, base_b = wide(own[:HALF]) + wide(from_left_a), wide(own[HALF:]) + wide(from_right_b)
    over_a, over_b, base_a, base_b = tie((over_a, over_b, base_a, base_b))
    from_right_a = shift_pool((wide(to_left_a) + wide(over_a)).astype(jnp.bfloat16), -1)
    from_left_b = shift_pool((wide(to_right_b) + wide(over_b)).astype(jnp.bfloat16), 1)
    summed = pl.pallas_call(
        sum_kernel,
        out_shape=jax.ShapeDtypeStruct(message, jnp.bfloat16),
        compiler_params=pltpu.CompilerParams(vmem_limit_bytes=BIG),
    )(base_a, base_b, from_right_a, from_left_b)
    returned = exchange(summed)
    layer_out = pl.pallas_call(
        finish_kernel,
        out_shape=jax.ShapeDtypeStruct((ROWS, D), jnp.bfloat16),
        compiler_params=pltpu.CompilerParams(vmem_limit_bytes=BIG),
    )(mix, returned, attended)
    return (attended, layer_out)


def solution(mesh):
    placed = (
        P(("pool", "ep"), None),
        P(("pool", "ep"), None),
        P(("pool", "ep"), None),
        P(("pool", "ep"), None),
        P(("pool", "ep"), None, None, None),
        P("ep", "pool", None, None, None),
        P(("pool", "ep"), None),
        P(("pool", "ep")),
        P(("pool", "ep")),
        P("ep", None),
        P(),
        P(("pool", "ep"), None),
        P(("pool", "ep"), None),
        P("ep", None, "pool"),
        P("ep", None, "pool"),
        P("ep", "pool", None),
    )
    return jax.shard_map(
        shards,
        mesh=mesh,
        in_specs=placed,
        out_specs=(P(("pool", "ep"), None), P(("pool", "ep"), None)),
        check_vma=False,
    )
```
